512 devices in a mesh: gx: 16 (over z, core), gy: 16 (over x, y_hi), sub: 2 (over y_lo).
Axes of the slice: x: 4, y: 8 (y_hi: 4, y_lo: 2; y = y_hi * 2 + y_lo), z: 8, core: 2. Of those that a mesh axis runs over, the one named last changes fastest.
Arguments:
- activity: float32 [128, 128, 128], P('gx', 'gy'), may hold values from 0.2 to 2
- anatomy: float32 [128, 128, 128], P('gx', 'gy'), may hold values from 0.2 to 2
- mr_data: float32 [128, 128, 128], P('gx', 'gy'), may hold values from 0.2 to 2
- sensitivity: float32 [128, 128, 128], P('gx', 'gy'), may hold values from 0.25 to 1
- blocks: bfloat16 [12288, 6, 128, 128], P(('gx', 'gy', 'sub')), may hold values from 9.9658966e-05 to 0.0025939941
- brick_ids: int32 [12288, 6], P(('gx', 'gy', 'sub')), may hold values from 0 to 1023, as said below
- counts: float32 [12288, 128], P(('gx', 'gy', 'sub')), may hold values from 0.2 to 5
- background: float32 [12288, 128], P(('gx', 'gy', 'sub')), may hold values from 0.2 to 1
Outputs:
- activity_next: float32 [128, 128, 128], P('gx', 'gy')
- anatomy_next: float32 [128, 128, 128], P('gx', 'gy')
The draws below stay inside these ranges and needn't reach their ends.
Inputs may be any that keep to these rules, and one draw needn't show every extreme that they name: `brick_ids`: an entry names a brick of its tile's row, numbered as gy * 64 + (local x * 8 + local y) * 1 + z block. The 6 bricks of one tile lie along a line: the same x and z block, at 6 consecutive values of y.
All inputs are finite; a program needn't handle non-finite values.
Results may differ from the reference program's by a relative error of at most 0.00042.
Values may be sent and summed in bfloat16 or wider, within the bound.
A program may use at most 64 MiB of HBM per device.

```python
import math
import jax
import jax.numpy as jnp
from jax import lax

CX = 8
CY = 8
CZ = 128
BRICK = 128
LORT = 128
K = 6
ITERS = 2
NX = 128
NY = 128
NBD = 64
TILES = 12288
N_GX = 16
N_GY = 16


def draw_brick_ids(key, part):
    key = jax.random.fold_in(key, 11)
    key_x, key_y, key_z = jax.random.split(key, 3)
    depth = CZ // BRICK
    tile_index = jnp.arange(TILES, dtype=jnp.int32)
    local_x = jax.random.randint(key_x, (TILES,), 0, CX, dtype=jnp.int32)
    start_y = jax.random.randint(key_y, (TILES,), 0, NY - K + 1, dtype=jnp.int32)
    z_block = jax.random.randint(key_z, (TILES,), 0, depth, dtype=jnp.int32)
    first = tile_index == 0
    last = tile_index == TILES - 1
    local_x = jnp.where(first, 0, jnp.where(last, CX - 1, local_x))
    start_y = jnp.where(first, 0, jnp.where(last, NY - K, start_y))
    z_block = jnp.where(first, 0, jnp.where(last, depth - 1, z_block))
    along = start_y[:, None] + jnp.arange(K, dtype=jnp.int32)[None, :]
    owner = along // CY
    inner_y = along % CY
    ids = owner * NBD + (local_x[:, None] * CY + inner_y) * depth + z_block[:, None]
    return ids.astype(jnp.int32)


def levels(own_key, dims, shards, smallest, high):
    def one(position, blocks):
        draws = jax.random.uniform(jax.random.fold_in(jax.random.fold_in(own_key, 6), position), (blocks,), jnp.float32, smallest / len(shards), high / len(shards))
        return jnp.repeat(jnp.exp(draws), dims[position] // blocks).reshape((-1,) + (1,) * (len(dims) - position - 1))

    factor_of = one(*shards[0])
    for cut in shards[1:]:
        factor_of = factor_of * one(*cut)
    return factor_of


def setup_inputs(seed: int = 0) -> dict:
    keys = jax.random.split(jax.random.key(seed), 9)
    return {
        "activity": jnp.clip(jnp.exp(math.log(2.0) - 2.3025851 * jax.random.uniform(keys[0], (NX, NY, CZ), jnp.float32) ** levels(keys[0], (NX, NY, CZ), ((0, 16), (1, 16)), -0.2, 0.2)), 0.2, 2.0),
        "anatomy": jnp.clip(jnp.exp(math.log(2.0) - 2.3025851 * jax.random.uniform(keys[1], (NX, NY, CZ), jnp.float32) ** levels(keys[1], (NX, NY, CZ), ((0, 16), (1, 16)), -0.2, 0.2)), 0.2, 2.0),
        "mr_data": jnp.clip(jnp.exp(math.log(2.0) - 2.3025851 * jax.random.uniform(keys[2], (NX, NY, CZ), jnp.float32) ** levels(keys[2], (NX, NY, CZ), ((0, 16), (1, 16)), -0.2, 0.2)), 0.2, 2.0),
        "sensitivity": jnp.clip(jnp.exp(math.log(1.0) - 1.3862944 * jax.random.uniform(keys[3], (NX, NY, CZ), jnp.float32) ** levels(keys[3], (NX, NY, CZ), ((0, 16), (1, 16)), -0.2, 0.2)), 0.25, 1.0),
        "blocks": jnp.clip(jnp.exp(math.log(0.0025939941) - 3.2592 * jax.random.uniform(keys[4], (TILES, K, LORT, BRICK), jnp.float32) ** levels(keys[4], (TILES, K, LORT, BRICK), ((0, 512),), -0.2, 0.2)), 9.965896606445312e-05, 0.0025939941).astype(jnp.bfloat16),
        "brick_ids": draw_brick_ids(jax.random.fold_in(keys[8], 71), 0),
        "counts": jnp.clip(jnp.exp(math.log(5.0) - 3.218876 * jax.random.uniform(keys[6], (TILES, LORT), jnp.float32) ** levels(keys[6], (TILES, LORT), ((0, 512),), -0.2, 0.2)), 0.2, 5.0),
        "background": jnp.clip(jnp.exp(math.log(1.0) - 1.609438 * jax.random.uniform(keys[7], (TILES, LORT), jnp.float32) ** levels(keys[7], (TILES, LORT), ((0, 512),), -0.2, 0.2)), 0.2, 1.0),
    }


EPSILON_SQ = 0.01
BETA = 0.2
TAU = 0.5
FLOOR = 0.05

def as_rows(field):
    shaped = field.reshape(N_GX, CX, N_GY, CY, CZ // BRICK, BRICK)
    return shaped.transpose(0, 2, 1, 3, 4, 5).reshape(N_GX, N_GY * CX * CY * (CZ // BRICK), BRICK)

def as_image(rows):
    shaped = rows.reshape(N_GX, N_GY, CX, CY, CZ // BRICK, BRICK)
    return shaped.transpose(0, 2, 1, 3, 4, 5).reshape(N_GX * CX, N_GY * CY, CZ)

def differences(field):
    along_x = jnp.concatenate([field[1:] - field[:-1], jnp.zeros_like(field[:1])], 0)
    along_y = jnp.concatenate([field[:, 1:] - field[:, :-1], jnp.zeros_like(field[:, :1])], 1)
    along_z = jnp.concatenate([field[:, :, 1:] - field[:, :, :-1], jnp.zeros_like(field[:, :, :1])], 2)
    return (along_x, along_y, along_z)

def fluxes(grad_act, grad_ana):
    cross_x = grad_act[1] * grad_ana[2] - grad_act[2] * grad_ana[1]
    cross_y = grad_act[2] * grad_ana[0] - grad_act[0] * grad_ana[2]
    cross_z = grad_act[0] * grad_ana[1] - grad_act[1] * grad_ana[0]
    inverse = 1.0 / jnp.sqrt(EPSILON_SQ + cross_x * cross_x + cross_y * cross_y + cross_z * cross_z)
    norm_act = grad_act[0] * grad_act[0] + grad_act[1] * grad_act[1] + grad_act[2] * grad_act[2]
    norm_ana = grad_ana[0] * grad_ana[0] + grad_ana[1] * grad_ana[1] + grad_ana[2] * grad_ana[2]
    inner = grad_act[0] * grad_ana[0] + grad_act[1] * grad_ana[1] + grad_act[2] * grad_ana[2]
    flux_act = tuple(((norm_ana * grad_act[d] - inner * grad_ana[d]) * inverse for d in range(3)))
    flux_ana = tuple(((norm_act * grad_ana[d] - inner * grad_act[d]) * inverse for d in range(3)))
    return (flux_act, flux_ana)

def divergence(flux):
    part_x = jnp.concatenate([jnp.zeros_like(flux[0][:1]), flux[0][:-1]], 0) - flux[0]
    part_y = jnp.concatenate([jnp.zeros_like(flux[1][:, :1]), flux[1][:, :-1]], 1) - flux[1]
    part_z = jnp.concatenate([jnp.zeros_like(flux[2][:, :, :1]), flux[2][:, :, :-1]], 2) - flux[2]
    return part_x + part_y + part_z

def project_row(inputs):
    row_bricks, block_vals, brick_list, measured, backdrop = inputs
    picked = row_bricks[brick_list]
    expected = jnp.einsum('tklj,tkj->tl', block_vals.astype(jnp.float32), picked.astype(jnp.float32)) + backdrop
    ratios = (1.0 - measured / expected).astype(jnp.bfloat16)
    backward = jnp.einsum('tklj,tl->tkj', block_vals.astype(jnp.float32), ratios.astype(jnp.float32))
    return jax.ops.segment_sum(backward.reshape(-1, BRICK), brick_list.reshape(-1), num_segments=row_bricks.shape[0])

def reference(activity, anatomy, mr_data, sensitivity, blocks, brick_ids, counts, background):
    block_rows = blocks.reshape(N_GX, -1, K, LORT, BRICK)
    id_rows = brick_ids.reshape(N_GX, -1, K)
    count_rows = counts.reshape(N_GX, -1, LORT)
    back_rows = background.reshape(N_GX, -1, LORT)
    current_act = activity
    current_ana = anatomy
    for repeat in range(ITERS):
        row_bricks = as_rows(current_act).astype(jnp.bfloat16)
        sums = lax.map(project_row, (row_bricks, block_rows, id_rows, count_rows, back_rows))
        data_grad = as_image(sums)
        flux_act, flux_ana = fluxes(differences(current_act), differences(current_ana))
        prior_act = divergence(flux_act)
        prior_ana = divergence(flux_ana)
        current_act = jnp.maximum(current_act - current_act / sensitivity * (data_grad + BETA * prior_act), FLOOR)
        current_ana = current_ana - TAU * (current_ana - mr_data + BETA * prior_ana)
    return (current_act, current_ana)
```

```python
import functools
import math

import jax
import jax.numpy as jnp
from jax import lax
from jax.experimental import pallas as pl
from jax.experimental.pallas import tpu as pltpu
from jax.sharding import PartitionSpec as P

ITERS = 2
EPSILON_SQ = 0.01
BETA = 0.2
TAU = 0.5
FLOOR = 0.05

MESH = pl.DeviceIdType.MESH
F32 = jnp.float32
BF16 = jnp.bfloat16

NCX, NCY = 4, 8
NGX, NGY = 16, 16
SLABS = 2 * NGX
TILES, K, LORT, BRICK = 24, 6, 128, 128
KP = 8
ENTRIES = TILES * KP
ENTRIES_PAD = 256
HALF = 32
QUAD = NCY * HALF

CODE_EPS = 1.0 / 64.0
CODE_MAX = 256.0
CODE_Q = 32766.0 / math.log1p(CODE_MAX / CODE_EPS)


def around(value, size):
    return lax.rem(value + size, size)


def offsets():
    every = [(a, b) for a in range(NCX) for b in range(NCY) if (a, b) != (0, 0)]
    return sorted(every, key=lambda p: -(min(p[0], NCX - p[0]) + min(p[1], NCY - p[1])))


OFFSETS = offsets()
INDEX = {p: i for i, p in enumerate(OFFSETS)}
NEAR_FIRST = OFFSETS[::-1]


def encode(x):
    code = jnp.log(1.0 + jnp.abs(x) * (1.0 / CODE_EPS)) * CODE_Q + 0.5
    code = jnp.minimum(code, 32767.0)
    return jnp.where(x < 0.0, -code, code).astype(jnp.int32).astype(jnp.int16)


def decode(code):
    value = code.astype(jnp.int32).astype(F32)
    size = (jnp.exp(jnp.abs(value) * (1.0 / CODE_Q)) - 1.0) * CODE_EPS
    return jnp.where(value < 0.0, -size, size)


def flux(gu, gv):
    cross_x = gu[1] * gv[2] - gu[2] * gv[1]
    cross_y = gu[2] * gv[0] - gu[0] * gv[2]
    cross_z = gu[0] * gv[1] - gu[1] * gv[0]
    inverse = 1.0 / jnp.sqrt(EPSILON_SQ + cross_x * cross_x + cross_y * cross_y + cross_z * cross_z)
    norm_u = gu[0] * gu[0] + gu[1] * gu[1] + gu[2] * gu[2]
    norm_v = gv[0] * gv[0] + gv[1] * gv[1] + gv[2] * gv[2]
    inner = gu[0] * gv[0] + gu[1] * gv[1] + gu[2] * gv[2]
    flux_u = [(norm_v * gu[d] - inner * gv[d]) * inverse for d in range(3)]
    flux_v = [(norm_u * gv[d] - inner * gu[d]) * inverse for d in range(3)]
    return flux_u, flux_v


def dot(a, b, dims):
    return lax.dot_general(a, b, (dims, ((), ())), preferred_element_type=F32)


NN = ((1,), (0,))
NT = ((1,), (1,))


def kernel(
    act_hbm, ana_hbm, mr_hbm, sens_hbm, blocks_hbm, ids_hbm, counts_hbm, back_hbm,
    u_out, v_out,
    u_ref, v_ref, mr_ref, sens_ref, blk, ids_ref, counts_ref, back_ref,
    gather_ref, scatter_ref, full, picked, expect, ratio, back_terms, own_part,
    send_b, recv_b, send_h, recv_h, strip,
    load_sem, a_send, a_recv, b_send, b_recv, h_send, h_recv, c_send, c_recv,
):
    gx = lax.axis_index("gx")
    gy = lax.axis_index("gy")
    sub = lax.axis_index("sub")
    cx, cy = gy // 4, (gy % 4) * 2 + sub
    slab = gx * 2 + sub

    def peer(a, b):
        x, y = lax.rem(cx + a, NCX), lax.rem(cy + b, NCY)
        return (gx, x * 4 + y // 2, lax.rem(y, 2))

    def neighbour(ds, dg):
        other = around(slab + ds, SLABS)
        return (other // 2, around(gy + dg, NGY), lax.rem(other, 2))

    barrier = pltpu.get_barrier_semaphore()
    side = 2 * sub - 1
    for a, b in OFFSETS:
        pl.semaphore_signal(barrier, inc=1, device_id=peer(a, b), device_id_type=MESH)
    pl.semaphore_signal(barrier, inc=1, device_id=neighbour(side, 0), device_id_type=MESH)
    pl.semaphore_signal(barrier, inc=1, device_id=neighbour(side, -side), device_id_type=MESH)

    mine = pl.ds(sub * 4, 4)
    loads = [
        pltpu.make_async_copy(act_hbm.at[mine], u_ref, load_sem.at[0]),
        pltpu.make_async_copy(ana_hbm.at[mine], v_ref, load_sem.at[1]),
        pltpu.make_async_copy(ids_hbm, ids_ref, load_sem.at[2]),
        pltpu.make_async_copy(blocks_hbm, blk, load_sem.at[3]),
        pltpu.make_async_copy(counts_hbm, counts_ref, load_sem.at[4]),
        pltpu.make_async_copy(back_hbm, back_ref, load_sem.at[5]),
        pltpu.make_async_copy(mr_hbm.at[mine], mr_ref, load_sem.at[6]),
        pltpu.make_async_copy(sens_hbm.at[mine], sens_ref, load_sem.at[7]),
    ]
    for load in loads:
        load.start()

    own_rows = pl.ds(pl.multiple_of(cy * HALF, HALF), HALF)
    row_id = lax.broadcasted_iota(jnp.int32, (8, BRICK), 0)
    lane_id = lax.broadcasted_iota(jnp.int32, (8, BRICK), 1)

    def share(phase):
        copies = []
        for a, b in OFFSETS:
            i = INDEX[a, b]
            copies.append(pltpu.make_async_remote_copy(
                src_ref=full.at[phase, 0, own_rows], dst_ref=full.at[phase, a, own_rows],
                send_sem=a_send.at[phase, i], recv_sem=a_recv.at[phase, i],
                device_id=peer(a, b), device_id_type=MESH))
        for copy in copies:
            copy.start()
        return copies

    def pack_halo(phase):
        for f, ref in enumerate((u_ref, v_ref)):
            send_h[phase, 0, f] = ref[0]
            send_h[phase, 1, f] = ref[3]
            for x in range(4):
                send_h[phase, 2, f, x:x + 1, :] = ref[x, 0:1, :]
                send_h[phase, 3, f, x:x + 1, :] = ref[x, 7:8, :]
            send_h[phase, 4, f, 0:1, :] = ref[3, 0:1, :]
            send_h[phase, 5, f, 0:1, :] = ref[0, 7:8, :]

    def share_halo(phase):
        copies = []
        for i, (ds, dg) in enumerate(((-1, 0), (1, 0), (0, -1), (0, 1), (1, -1), (-1, 1))):
            copies.append(pltpu.make_async_remote_copy(
                src_ref=send_h.at[phase, i], dst_ref=recv_h.at[phase, i],
                send_sem=h_send.at[phase, i], recv_sem=h_recv.at[phase, i],
                device_id=neighbour(ds, dg), device_id_type=MESH))
        for copy in copies:
            copy.start()
        return copies

    def gather_bricks(phase, copies):
        total = None
        for a in (0, 1, 3, 2):
            for b in range(NCY):
                if (a, b) != (0, 0):
                    copies[INDEX[a, b]].wait_recv()
            part = dot(gather_ref[a], full[phase, a], NN)
            total = part if total is None else total + part
        picked[...] = total.reshape(TILES, KP, BRICK)

    def only_row(values, k):
        return jnp.where(row_id == k, values, 0.0).astype(BF16)

    def project(step, carry):
        for sub_step in range(4):
            t = step * 4 + sub_step
            x = picked[t]
            total = None
            lhs = jnp.concatenate([only_row(x, k) for k in range(K)], axis=1)
            rhs = jnp.concatenate([blk[t, k] for k in range(K)], axis=1)
            total = dot(lhs, rhs, NT)
            expect[pl.ds(t, 1), :] = jnp.sum(total, axis=0, keepdims=True)
        return carry

    def backproject(step, carry):
        for sub_step in range(4):
            t = step * 4 + sub_step
            r = jnp.broadcast_to(ratio[pl.ds(t, 1), :], (8, LORT))
            lhs = jnp.concatenate([only_row(r, k) for k in range(K)], axis=1)
            back_terms[t] = dot(lhs, blk[t].reshape(K * LORT, BRICK), NN)
        return carry

    def scatter_and_send(phase):
        terms = back_terms[...].reshape(ENTRIES_PAD, BRICK)
        high = terms.astype(BF16)
        low = (terms - high.astype(F32)).astype(BF16)
        copies = [None] * len(OFFSETS)
        for a in (2, 1, 3, 0):
            part = dot(scatter_ref[a], high, NN) + dot(scatter_ref[a], low, NN)
            send_b[phase, a] = encode(part)
            if a == 0:
                own_part[...] = part
            for x, b in OFFSETS:
                if x != a:
                    continue
                i = INDEX[a, b]
                rows = pl.ds(pl.multiple_of(lax.rem(cy + b, NCY) * HALF, HALF), HALF)
                copies[i] = pltpu.make_async_remote_copy(
                    src_ref=send_b.at[phase, a, rows], dst_ref=recv_b.at[phase, i],
                    send_sem=b_send.at[phase, i], recv_sem=b_recv.at[phase, i],
                    device_id=peer(a, b), device_id_type=MESH)
                copies[i].start()
        return copies

    def summed_gradient(phase, copies):
        total = own_part[own_rows, :]
        for p in NEAR_FIRST:
            i = INDEX[p]
            copies[i].wait_recv()
            total = total + decode(recv_b[phase, i])
        return total.reshape(4, 8, BRICK)

    first_slab, last_slab = slab == 0, slab == SLABS - 1
    first_gy, last_gy = gy == 0, gy == NGY - 1

    def prior(phase, copies):
        for copy in copies:
            copy.wait_recv()

        def layers(f, ref):
            return [recv_h[phase, 1, f]] + [ref[x] for x in range(4)] + [recv_h[phase, 0, f]]

        def depth(f):
            return jnp.where(lane_id < BRICK - 1, pltpu.roll(f, BRICK - 1, 1) - f, 0.0)

        def gradient(all_layers, f, x):
            here, after = all_layers[x], all_layers[x + 1]
            along_x = after - here
            if x == 4:
                along_x = jnp.where(last_slab, 0.0, along_x)
            row = recv_h[phase, 4, f, 0:1, :] if x == 0 else recv_h[phase, 2, f, x - 1:x, :]
            shifted = jnp.where(row_id < 7, pltpu.roll(here, 7, 0), jnp.broadcast_to(row, (8, BRICK)))
            along_y = jnp.where(jnp.logical_and(last_gy, row_id == 7), 0.0, shifted - here)
            return along_x, along_y, depth(here)

        def before_gradient(f):
            here = recv_h[phase, 3, f]
            after = recv_h[phase, 5, f, 0:1, :]
            shifted = jnp.where(row_id < 3, pltpu.roll(here, 7, 0), jnp.broadcast_to(after, (8, BRICK)))
            along_x = jnp.where(jnp.logical_and(last_slab, row_id == 3), 0.0, shifted - here)
            return along_x, send_h[phase, 2, f] - here, depth(here)

        us, vs = layers(0, u_ref), layers(1, v_ref)
        parts = [flux(gradient(us, 0, x), gradient(vs, 1, x)) for x in range(5)]
        before = flux(before_gradient(0), before_gradient(1))
        result = []
        for f in range(2):
            strip[f] = before[f][1]
            found = []
            for x in range(1, 5):
                now = parts[x][f]
                prev_x = parts[x - 1][f][0]
                if x == 1:
                    prev_x = jnp.where(first_slab, 0.0, prev_x)
                row = jnp.broadcast_to(strip[f, x - 1:x, :], (8, BRICK))
                row = jnp.where(first_gy, 0.0, row)
                prev_y = jnp.where(row_id > 0, pltpu.roll(now[1], 1, 0), row)
                prev_z = jnp.where(lane_id > 0, pltpu.roll(now[2], 1, 1), 0.0)
                found.append((prev_x - now[0]) + (prev_y - now[1]) + (prev_z - now[2]))
            result.append(found)
        return result

    loads[2].wait()
    ids = ids_ref[...]
    lane6 = lax.broadcasted_iota(jnp.int32, (TILES, KP, K), 2)
    k_of = lax.broadcasted_iota(jnp.int32, (TILES, KP, K), 1)
    spread = jnp.where(lane6 == k_of, jnp.broadcast_to(ids.reshape(TILES, 1, K), (TILES, KP, K)) + 1, 0)
    column = jnp.sum(spread.astype(F32), axis=2, keepdims=True) - 1.0
    column = column.astype(jnp.int32)
    entry = (lax.broadcasted_iota(jnp.int32, (TILES, KP, ENTRIES_PAD), 0) * KP
             + lax.broadcasted_iota(jnp.int32, (TILES, KP, ENTRIES_PAD), 1))
    lanes = lax.broadcasted_iota(jnp.int32, (TILES, KP, ENTRIES_PAD), 2)
    as_row = jnp.where(entry == lanes, column + 1, 0).astype(F32)
    as_row = jnp.sum(jnp.sum(as_row, axis=0), axis=0, keepdims=True).astype(jnp.int32) - 1
    bricks = lax.broadcasted_iota(jnp.int32, (QUAD, ENTRIES_PAD), 0)
    for a in range(NCX):
        came_from = around(cx - a, NCX) * QUAD
        goes_to = lax.rem(cx + a, NCX) * QUAD
        gather_ref[a] = jnp.where(lanes + came_from == column, 1.0, 0.0).reshape(ENTRIES, QUAD).astype(BF16)
        scatter_ref[a] = jnp.where(bricks + goes_to == as_row, 1.0, 0.0).astype(BF16)
    back_terms[pl.ds(TILES, ENTRIES_PAD // KP - TILES)] = jnp.zeros((ENTRIES_PAD // KP - TILES, KP, BRICK), F32)
    send_h[...] = jnp.zeros_like(send_h)
    loads[0].wait()
    loads[1].wait()
    full[0, 0, own_rows, :] = u_ref[...].reshape(HALF, BRICK).astype(BF16)
    pack_halo(0)

    pl.semaphore_wait(barrier, len(OFFSETS) + 2)

    pending = []
    for phase in range(ITERS):
        shared = share(phase)
        halo = share_halo(phase)
        pending += shared + halo
        if phase == 0:
            for i in (3, 4, 5, 6, 7):
                loads[i].wait()
        gather_bricks(phase, shared)
        lax.fori_loop(0, TILES // 4, project, 0)
        ratio[...] = 1.0 - counts_ref[...] / (expect[...] + back_ref[...])
        lax.fori_loop(0, TILES // 4, backproject, 0)
        sent = scatter_and_send(phase)
        pending += sent
        prior_u, prior_v = prior(phase, halo)
        gradient = summed_gradient(phase, sent)
        last = phase == ITERS - 1
        for x in range(4):
            u, v = u_ref[x], v_ref[x]
            new_u = jnp.maximum(u - u / sens_ref[x] * (gradient[x] + BETA * prior_u[x]), FLOOR)
            new_v = v - TAU * (v - mr_ref[x] + BETA * prior_v[x])
            if last:
                u_out[sub * 4 + x] = new_u
                v_out[sub * 4 + x] = new_v
            else:
                u_ref[x] = new_u
                v_ref[x] = new_v
        if not last:
            full[phase + 1, 0, own_rows, :] = u_ref[...].reshape(HALF, BRICK).astype(BF16)
            pack_halo(phase + 1)

    partner = (gx, gy, 1 - sub)
    for i, out in enumerate((u_out, v_out)):
        copy = pltpu.make_async_remote_copy(
            src_ref=out.at[mine], dst_ref=out.at[mine],
            send_sem=c_send.at[i], recv_sem=c_recv.at[i], device_id=partner, device_id_type=MESH)
        copy.start()
        pending.append(copy)
    pending[-1].wait_recv()
    pending[-2].wait_recv()
    for copy in pending:
        copy.wait_send()


def local(activity, anatomy, mr_data, sensitivity, blocks, brick_ids, counts, background):
    n = len(OFFSETS)
    any_space = pl.BlockSpec(memory_space=pl.ANY)
    vmem = pl.BlockSpec(memory_space=pltpu.VMEM)
    half = (4, 8, BRICK)
    dma = pltpu.SemaphoreType.DMA
    return pl.pallas_call(
        kernel,
        out_shape=(jax.ShapeDtypeStruct(activity.shape, F32), jax.ShapeDtypeStruct(anatomy.shape, F32)),
        in_specs=[any_space] * 8,
        out_specs=(vmem, vmem),
        scratch_shapes=[
            pltpu.VMEM(half, F32), pltpu.VMEM(half, F32), pltpu.VMEM(half, F32), pltpu.VMEM(half, F32),
            pltpu.VMEM(blocks.shape, BF16),
            pltpu.VMEM(brick_ids.shape, jnp.int32),
            pltpu.VMEM(counts.shape, F32), pltpu.VMEM(background.shape, F32),
            pltpu.VMEM((NCX, ENTRIES, QUAD), BF16),
            pltpu.VMEM((NCX, QUAD, ENTRIES_PAD), BF16),
            pltpu.VMEM((ITERS, NCX, QUAD, BRICK), BF16),
            pltpu.VMEM((TILES, KP, BRICK), F32),
            pltpu.VMEM((TILES, LORT), F32),
            pltpu.VMEM((TILES, LORT), F32),
            pltpu.VMEM((ENTRIES_PAD // KP, KP, BRICK), F32),
            pltpu.VMEM((QUAD, BRICK), F32),
            pltpu.VMEM((ITERS, NCX, QUAD, BRICK), jnp.int16),
            pltpu.VMEM((ITERS, n, HALF, BRICK), jnp.int16),
            pltpu.VMEM((ITERS, 6, 2, 8, BRICK), F32),
            pltpu.VMEM((ITERS, 6, 2, 8, BRICK), F32),
            pltpu.VMEM((2, 8, BRICK), F32),
            dma((8,)), dma((ITERS, n)), dma((ITERS, n)), dma((ITERS, n)), dma((ITERS, n)),
            dma((ITERS, 6)), dma((ITERS, 6)), dma((2,)), dma((2,)),
        ],
        compiler_params=pltpu.CompilerParams(
            collective_id=0, has_side_effects=True, vmem_limit_bytes=24 * 1024 * 1024),
    )(activity, anatomy, mr_data, sensitivity, blocks, brick_ids, counts, background)


def solution(mesh):
    image = P("gx", "gy", None)
    tiles = ("gx", "gy", "sub")
    in_specs = (image, image, image, image, P(tiles, None, None, None), P(tiles, None), P(tiles, None), P(tiles, None))
    return jax.shard_map(local, mesh=mesh, in_specs=in_specs, out_specs=(image, image), check_vma=False)
```

```python
import functools
import math

import jax
import jax.numpy as jnp
from jax import lax
from jax.experimental import pallas as pl
from jax.experimental.pallas import tpu as pltpu
from jax.sharding import PartitionSpec as P

ITERS = 2
EPSILON_SQ = 0.01
BETA = 0.2
TAU = 0.5
FLOOR = 0.05

MESH = pl.DeviceIdType.MESH
F32 = jnp.float32
BF16 = jnp.bfloat16

NCX, NCY = 4, 8
NGX, NGY = 16, 16
SLABS = 2 * NGX
TILES, K, LORT, BRICK = 24, 6, 128, 128
TOGETHER = 12
KP = 8
ENTRIES = TILES * KP
ENTRIES_PAD = 256
HALF = 32
QUAD = NCY * HALF

CODE_EPS = 1.0 / 64.0
CODE_MAX = 256.0
CODE_Q = 32766.0 / math.log1p(CODE_MAX / CODE_EPS)


def around(value, size):
    return lax.rem(value + size, size)


def offsets():
    every = [(a, b) for a in range(NCX) for b in range(NCY) if (a, b) != (0, 0)]
    return sorted(every, key=lambda p: -(min(p[0], NCX - p[0]) + min(p[1], NCY - p[1])))


OFFSETS = offsets()
INDEX = {p: i for i, p in enumerate(OFFSETS)}
NEAR_FIRST = OFFSETS[::-1]


HALOS = ((-1, 0), (1, 0), (0, -1), (0, 1), (1, -1), (-1, 1))


def encode(x):
    code = jnp.log(1.0 + jnp.abs(x) * (1.0 / CODE_EPS)) * CODE_Q + 0.5
    code = jnp.minimum(code, 32767.0)
    return jnp.where(x < 0.0, -code, code).astype(jnp.int32).astype(jnp.int16)


def decode(code):
    value = code.astype(jnp.int32).astype(F32)
    size = (jnp.exp(jnp.abs(value) * (1.0 / CODE_Q)) - 1.0) * CODE_EPS
    return jnp.where(value < 0.0, -size, size)


def flux(gu, gv):
    cross_x = gu[1] * gv[2] - gu[2] * gv[1]
    cross_y = gu[2] * gv[0] - gu[0] * gv[2]
    cross_z = gu[0] * gv[1] - gu[1] * gv[0]
    inverse = 1.0 / jnp.sqrt(EPSILON_SQ + cross_x * cross_x + cross_y * cross_y + cross_z * cross_z)
    norm_u = gu[0] * gu[0] + gu[1] * gu[1] + gu[2] * gu[2]
    norm_v = gv[0] * gv[0] + gv[1] * gv[1] + gv[2] * gv[2]
    inner = gu[0] * gv[0] + gu[1] * gv[1] + gu[2] * gv[2]
    flux_u = [(norm_v * gu[d] - inner * gv[d]) * inverse for d in range(3)]
    flux_v = [(norm_u * gv[d] - inner * gu[d]) * inverse for d in range(3)]
    return flux_u, flux_v


def dot(a, b, dims):
    return lax.dot_general(a, b, (dims, ((), ())), preferred_element_type=F32)


NN = ((1,), (0,))
NT = ((1,), (1,))


def kernel(
    act_hbm, ana_hbm, mr_hbm, sens_hbm, blocks_hbm, ids_hbm, counts_hbm, back_hbm,
    u_out, v_out,
    u_ref, v_ref, mr_ref, sens_ref, blk, ids_ref, counts_ref, back_ref,
    gather_ref, scatter_ref, full, picked, expect, ratio, back_terms, own_part,
    send_b, recv_b, send_h, recv_h, strip,
    load_sem, a_send, a_recv, b_send, b_recv, h_send, h_recv, c_send, c_recv, across_sem,
):
    gx = lax.axis_index("gx")
    gy = lax.axis_index("gy")
    sub = lax.axis_index("sub")
    cx, cy = gy // 4, (gy % 4) * 2 + sub
    slab = gx * 2 + sub

    def peer(a, b):
        x, y = lax.rem(cx + a, NCX), lax.rem(cy + b, NCY)
        return (gx, x * 4 + y // 2, lax.rem(y, 2))

    def neighbour(ds, dg):
        other = around(slab + ds, SLABS)
        return (other // 2, around(gy + dg, NGY), lax.rem(other, 2))

    barrier = pltpu.get_barrier_semaphore()
    first_slab, last_slab = slab == 0, slab == SLABS - 1
    first_gy, last_gy = gy == 0, gy == NGY - 1
    side = 2 * sub - 1
    across = (neighbour(side, 0), neighbour(side, -side))
    before_next = jnp.logical_and(sub == 1, jnp.logical_not(last_slab))
    after_last = jnp.logical_and(sub == 0, jnp.logical_not(first_slab))
    for a, b in OFFSETS:
        pl.semaphore_signal(barrier, inc=1, device_id=peer(a, b), device_id_type=MESH)

    @pl.when(before_next)
    def _():
        for device in across:
            pl.semaphore_signal(barrier, inc=1, device_id=device, device_id_type=MESH)

    mine = pl.ds(sub * 4, 4)
    loads = [
        pltpu.make_async_copy(act_hbm.at[mine], u_ref, load_sem.at[0]),
        pltpu.make_async_copy(ana_hbm.at[mine], v_ref, load_sem.at[1]),
        pltpu.make_async_copy(ids_hbm, ids_ref, load_sem.at[2]),
        pltpu.make_async_copy(blocks_hbm, blk, load_sem.at[3]),
        pltpu.make_async_copy(counts_hbm, counts_ref, load_sem.at[4]),
        pltpu.make_async_copy(back_hbm, back_ref, load_sem.at[5]),
        pltpu.make_async_copy(mr_hbm.at[mine], mr_ref, load_sem.at[6]),
        pltpu.make_async_copy(sens_hbm.at[mine], sens_ref, load_sem.at[7]),
    ]
    for load in loads:
        load.start()

    own_rows = pl.ds(pl.multiple_of(cy * HALF, HALF), HALF)
    row_id = lax.broadcasted_iota(jnp.int32, (8, BRICK), 0)
    lane_id = lax.broadcasted_iota(jnp.int32, (8, BRICK), 1)

    def share(phase):
        copies = []
        for a, b in OFFSETS:
            i = INDEX[a, b]
            copies.append(pltpu.make_async_remote_copy(
                src_ref=full.at[phase, 0, own_rows], dst_ref=full.at[phase, a, own_rows],
                send_sem=a_send.at[phase, i], recv_sem=a_recv.at[phase, i],
                device_id=peer(a, b), device_id_type=MESH))
        for copy in copies:
            copy.start()
        return copies

    def pack_halo(phase):
        for f, ref in enumerate((u_ref, v_ref)):
            send_h[phase, 0, f] = ref[0]
            send_h[phase, 1, f] = ref[3]
            for x in range(4):
                send_h[phase, 2, f, x:x + 1, :] = ref[x, 0:1, :]
                send_h[phase, 3, f, x:x + 1, :] = ref[x, 7:8, :]
            send_h[phase, 4, f, 0:1, :] = ref[3, 0:1, :]
            send_h[phase, 5, f, 0:1, :] = ref[0, 7:8, :]

    def halo_copies(phase):
        copies = []
        for i, (ds, dg) in enumerate(HALOS):
            copies.append(pltpu.make_async_remote_copy(
                src_ref=send_h.at[phase, i], dst_ref=recv_h.at[phase, i],
                send_sem=h_send.at[phase, i], recv_sem=h_recv.at[phase, i],
                device_id=neighbour(ds, dg), device_id_type=MESH))
        return copies

    def goes(i):
        ds = HALOS[i][0]
        return None if ds == 0 else jnp.logical_not(last_slab if ds > 0 else first_slab)

    def comes(i):
        ds = HALOS[i][0]
        return None if ds == 0 else jnp.logical_not(first_slab if ds > 0 else last_slab)

    def only_if(condition, act):
        if condition is None:
            act()
        else:
            pl.when(condition)(act)

    def start_halo(copies, condition=None):
        for i, copy in enumerate(copies):
            terms = [c for c in (condition, goes(i)) if c is not None]
            only_if(functools.reduce(jnp.logical_and, terms) if terms else None, copy.start)

    def gather_bricks(phase, copies):
        total = None
        for a in (0, 1, 3, 2):
            for b in range(NCY):
                if (a, b) != (0, 0):
                    copies[INDEX[a, b]].wait_recv()
            part = dot(gather_ref[a], full[phase, a], NN)
            total = part if total is None else total + part
        picked[...] = total.reshape(TILES, KP, BRICK)

    def only_row(values, k):
        return jnp.where(row_id == k, values, 0.0).astype(BF16)

    def project(step, carry):
        for inner in range(TOGETHER):
            t = step * TOGETHER + inner
            x = picked[t]
            lhs = jnp.concatenate([only_row(x, k) for k in range(K)], axis=1)
            rhs = jnp.concatenate([blk[t, k] for k in range(K)], axis=1)
            total = dot(lhs, rhs, NT)
            expect[pl.ds(t, 1), :] = jnp.sum(total, axis=0, keepdims=True)
        return carry

    def backproject(step, carry):
        for inner in range(TOGETHER):
            t = step * TOGETHER + inner
            r = jnp.broadcast_to(ratio[pl.ds(t, 1), :], (8, LORT))
            lhs = jnp.concatenate([only_row(r, k) for k in range(K)], axis=1)
            back_terms[t] = dot(lhs, blk[t].reshape(K * LORT, BRICK), NN)
        return carry

    def scatter_and_send(phase):
        terms = back_terms[...].reshape(ENTRIES_PAD, BRICK)
        high = terms.astype(BF16)
        low = (terms - high.astype(F32)).astype(BF16)
        copies = [None] * len(OFFSETS)
        for a in (2, 1, 3, 0):
            part = dot(scatter_ref[a], high, NN) + dot(scatter_ref[a], low, NN)
            send_b[phase, a] = encode(part)
            if a == 0:
                own_part[...] = part
            for x, b in OFFSETS:
                if x != a:
                    continue
                i = INDEX[a, b]
                rows = pl.ds(pl.multiple_of(lax.rem(cy + b, NCY) * HALF, HALF), HALF)
                copies[i] = pltpu.make_async_remote_copy(
                    src_ref=send_b.at[phase, a, rows], dst_ref=recv_b.at[phase, i],
                    send_sem=b_send.at[phase, i], recv_sem=b_recv.at[phase, i],
                    device_id=peer(a, b), device_id_type=MESH)
                copies[i].start()
        return copies

    def summed_gradient(phase, copies):
        total = own_part[own_rows, :]
        for p in NEAR_FIRST:
            i = INDEX[p]
            copies[i].wait_recv()
            total = total + decode(recv_b[phase, i])
        return total.reshape(4, 8, BRICK)

    def prior(phase, copies):
        for i, copy in enumerate(copies):
            only_if(comes(i), copy.wait_recv)

        def layers(f, ref):
            return [recv_h[phase, 1, f]] + [ref[x] for x in range(4)] + [recv_h[phase, 0, f]]

        def depth(f):
            return jnp.where(lane_id < BRICK - 1, pltpu.roll(f, BRICK - 1, 1) - f, 0.0)

        def gradient(all_layers, f, x):
            here, after = all_layers[x], all_layers[x + 1]
            along_x = after - here
            if x == 4:
                along_x = jnp.where(last_slab, 0.0, along_x)
            row = recv_h[phase, 4, f, 0:1, :] if x == 0 else recv_h[phase, 2, f, x - 1:x, :]
            shifted = jnp.where(row_id < 7, pltpu.roll(here, 7, 0), jnp.broadcast_to(row, (8, BRICK)))
            along_y = jnp.where(jnp.logical_and(last_gy, row_id == 7), 0.0, shifted - here)
            return along_x, along_y, depth(here)

        def before_gradient(f):
            here = recv_h[phase, 3, f]
            after = recv_h[phase, 5, f, 0:1, :]
            shifted = jnp.where(row_id < 3, pltpu.roll(here, 7, 0), jnp.broadcast_to(after, (8, BRICK)))
            along_x = jnp.where(jnp.logical_and(last_slab, row_id == 3), 0.0, shifted - here)
            return along_x, send_h[phase, 2, f] - here, depth(here)

        us, vs = layers(0, u_ref), layers(1, v_ref)
        parts = [flux(gradient(us, 0, x), gradient(vs, 1, x)) for x in range(5)]
        before = flux(before_gradient(0), before_gradient(1))
        result = []
        for f in range(2):
            strip[f] = before[f][1]
            found = []
            for x in range(1, 5):
                now = parts[x][f]
                prev_x = parts[x - 1][f][0]
                if x == 1:
                    prev_x = jnp.where(first_slab, 0.0, prev_x)
                row = jnp.broadcast_to(strip[f, x - 1:x, :], (8, BRICK))
                row = jnp.where(first_gy, 0.0, row)
                prev_y = jnp.where(row_id > 0, pltpu.roll(now[1], 1, 0), row)
                prev_z = jnp.where(lane_id > 0, pltpu.roll(now[2], 1, 1), 0.0)
                found.append((prev_x - now[0]) + (prev_y - now[1]) + (prev_z - now[2]))
            result.append(found)
        return result

    loads[2].wait()
    entry_t = lax.broadcasted_iota(jnp.int32, (TILES, KP, ENTRIES_PAD), 0)
    entry_k = lax.broadcasted_iota(jnp.int32, (TILES, KP, ENTRIES_PAD), 1)
    lanes = lax.broadcasted_iota(jnp.int32, (TILES, KP, ENTRIES_PAD), 2)
    by_tile = jnp.concatenate([ids_ref[...], jnp.zeros((KP - K, TILES), jnp.int32)], axis=0).astype(F32)
    tile_lane = lax.broadcasted_iota(jnp.int32, (TILES, KP, TILES), 2)
    tile_of = lax.broadcasted_iota(jnp.int32, (TILES, KP, TILES), 0)
    k_of = lax.broadcasted_iota(jnp.int32, (TILES, KP, TILES), 1)
    chosen = jnp.logical_and(tile_lane == tile_of, k_of < K)
    column = jnp.sum(jnp.where(chosen, by_tile[None] + 1.0, 0.0), axis=2, keepdims=True)
    as_row = jnp.where(entry_t * KP + entry_k == lanes, column, 0.0)
    as_row = jnp.sum(jnp.sum(as_row, axis=0), axis=0, keepdims=True).astype(jnp.int32) - 1
    column = column.astype(jnp.int32) - 1
    bricks = lax.broadcasted_iota(jnp.int32, (QUAD, ENTRIES_PAD), 0)
    for a in range(NCX):
        came_from = around(cx - a, NCX) * QUAD
        goes_to = lax.rem(cx + a, NCX) * QUAD
        gather_ref[a] = jnp.where(lanes + came_from == column, 1.0, 0.0).reshape(ENTRIES, QUAD).astype(BF16)
        scatter_ref[a] = jnp.where(bricks + goes_to == as_row, 1.0, 0.0).astype(BF16)
    back_terms[pl.ds(TILES, ENTRIES_PAD // KP - TILES)] = jnp.zeros((ENTRIES_PAD // KP - TILES, KP, BRICK), F32)
    send_h[...] = jnp.zeros_like(send_h)
    loads[0].wait()
    loads[1].wait()
    full[0, 0, own_rows, :] = u_ref[...].reshape(HALF, BRICK).astype(BF16)

    @pl.when(jnp.logical_not(after_last))
    def _():
        pl.semaphore_wait(barrier, len(OFFSETS))

    @pl.when(after_last)
    def _():
        pl.semaphore_wait(barrier, len(OFFSETS) + len(across))
        for device in across:
            pl.semaphore_signal(across_sem, inc=1, device_id=device, device_id_type=MESH)

    def swap(i, out):
        copy = pltpu.make_async_remote_copy(
            src_ref=out.at[mine], dst_ref=out.at[mine],
            send_sem=c_send.at[i], recv_sem=c_recv.at[i], device_id=(gx, gy, 1 - sub), device_id_type=MESH)
        copy.start()
        return copy

    pending, halos = [], []
    for phase in range(ITERS):
        shared = share(phase)
        pack_halo(phase)
        halo = halo_copies(phase)
        if phase == 0:
            start_halo(halo, jnp.logical_not(before_next))
        else:
            start_halo(halo)
        if phase == 0:
            for i in (3, 4, 5, 6, 7):
                loads[i].wait()
        gather_bricks(phase, shared)
        if phase == 0:
            @pl.when(before_next)
            def _():
                pl.semaphore_wait(across_sem, len(across))

            start_halo(halo, before_next)
        lax.fori_loop(0, TILES // TOGETHER, project, 0)
        ratio[...] = 1.0 - counts_ref[...] / (expect[...] + back_ref[...])
        lax.fori_loop(0, TILES // TOGETHER, backproject, 0)
        sent = scatter_and_send(phase)
        pending += shared + sent
        halos += halo
        prior_u, prior_v = prior(phase, halo)
        last = phase == ITERS - 1
        step = [u_ref[x] / sens_ref[x] for x in range(4)]
        for x in range(4):
            v = v_ref[x]
            new_v = v - TAU * (v - mr_ref[x] + BETA * prior_v[x])
            if last:
                v_out[sub * 4 + x] = new_v
            else:
                v_ref[x] = new_v
        if last:
            swaps = [swap(1, v_out)]
        gradient = summed_gradient(phase, sent)
        for x in range(4):
            new_u = jnp.maximum(u_ref[x] - step[x] * (gradient[x] + BETA * prior_u[x]), FLOOR)
            if last:
                u_out[sub * 4 + x] = new_u
            else:
                u_ref[x] = new_u
        if not last:
            full[phase + 1, 0, own_rows, :] = u_ref[...].reshape(HALF, BRICK).astype(BF16)

    swaps.append(swap(0, u_out))
    for copy in swaps:
        copy.wait_recv()
    pending += swaps
    for copy in pending:
        copy.wait_send()
    for i, copy in enumerate(halos):
        only_if(goes(i % len(HALOS)), copy.wait_send)


def local(activity, anatomy, mr_data, sensitivity, blocks, brick_ids, counts, background):
    n = len(OFFSETS)
    hbm = pl.BlockSpec(memory_space=pltpu.HBM)
    vmem = pl.BlockSpec(memory_space=pltpu.VMEM)
    half = (4, 8, BRICK)
    dma = pltpu.SemaphoreType.DMA
    operands = (activity, anatomy, mr_data, sensitivity, blocks, brick_ids.T, counts, background)
    return pl.pallas_call(
        kernel,
        out_shape=(jax.ShapeDtypeStruct(activity.shape, F32), jax.ShapeDtypeStruct(anatomy.shape, F32)),
        in_specs=[hbm] * 8,
        out_specs=(vmem, vmem),
        scratch_shapes=[
            pltpu.VMEM(half, F32), pltpu.VMEM(half, F32), pltpu.VMEM(half, F32), pltpu.VMEM(half, F32),
            pltpu.VMEM(blocks.shape, BF16),
            pltpu.VMEM((K, TILES), jnp.int32),
            pltpu.VMEM(counts.shape, F32), pltpu.VMEM(background.shape, F32),
            pltpu.VMEM((NCX, ENTRIES, QUAD), BF16),
            pltpu.VMEM((NCX, QUAD, ENTRIES_PAD), BF16),
            pltpu.VMEM((ITERS, NCX, QUAD, BRICK), BF16),
            pltpu.VMEM((TILES, KP, BRICK), F32),
            pltpu.VMEM((TILES, LORT), F32),
            pltpu.VMEM((TILES, LORT), F32),
            pltpu.VMEM((ENTRIES_PAD // KP, KP, BRICK), F32),
            pltpu.VMEM((QUAD, BRICK), F32),
            pltpu.VMEM((ITERS, NCX, QUAD, BRICK), jnp.int16),
            pltpu.VMEM((ITERS, n, HALF, BRICK), jnp.int16),
            pltpu.VMEM((ITERS, 6, 2, 8, BRICK), F32),
            pltpu.VMEM((ITERS, 6, 2, 8, BRICK), F32),
            pltpu.VMEM((2, 8, BRICK), F32),
            dma((8,)), dma((ITERS, n)), dma((ITERS, n)), dma((ITERS, n)), dma((ITERS, n)),
            dma((ITERS, 6)), dma((ITERS, 6)), dma((2,)), dma((2,)), pltpu.SemaphoreType.REGULAR,
        ],
        compiler_params=pltpu.CompilerParams(
            collective_id=0, has_side_effects=True, vmem_limit_bytes=32 * 1024 * 1024),
    )(*[pltpu.with_memory_space_constraint(x, pltpu.HBM) for x in operands])


def solution(mesh):
    image = P("gx", "gy", None)
    tiles = ("gx", "gy", "sub")
    in_specs = (image, image, image, image, P(tiles, None, None, None), P(tiles, None), P(tiles, None), P(tiles, None))
    return jax.shard_map(local, mesh=mesh, in_specs=in_specs, out_specs=(image, image), check_vma=False)
```

```python
import functools
import math

import jax
import jax.numpy as jnp
from jax import lax
from jax.experimental import pallas as pl
from jax.experimental.pallas import tpu as pltpu
from jax.sharding import PartitionSpec as P

ITERS = 2
EPSILON_SQ = 0.01
BETA = 0.2
TAU = 0.5
FLOOR = 0.05

MESH = pl.DeviceIdType.MESH
F32 = jnp.float32
BF16 = jnp.bfloat16

NCX, NCY = 4, 8
NGX, NGY = 16, 16
SLABS = 2 * NGX
TILES, K, LORT, BRICK = 24, 6, 128, 128
TOGETHER = 12
KP = 8
ENTRIES = TILES * KP
ENTRIES_PAD = 256
HALF = 32
QUAD = NCY * HALF

CODE_EPS = 1.0 / 64.0
CODE_MAX = 256.0
CODE_Q = 32766.0 / math.log1p(CODE_MAX / CODE_EPS)


def around(value, size):
    return lax.rem(value + size, size)


def offsets():
    every = [(a, b) for a in range(NCX) for b in range(NCY) if (a, b) != (0, 0)]
    return sorted(every, key=lambda p: -(min(p[0], NCX - p[0]) + min(p[1], NCY - p[1])))


OFFSETS = offsets()


HALOS = ((-1, 0), (1, 0), (0, -1), (0, 1), (1, -1), (-1, 1))


def encode(x):
    code = jnp.log(1.0 + jnp.abs(x) * (1.0 / CODE_EPS)) * CODE_Q + 0.5
    code = jnp.minimum(code, 32767.0)
    return jnp.where(x < 0.0, -code, code).astype(jnp.int32).astype(jnp.int16)


def decode(code):
    value = code.astype(jnp.int32).astype(F32)
    size = (jnp.exp(jnp.abs(value) * (1.0 / CODE_Q)) - 1.0) * CODE_EPS
    return jnp.where(value < 0.0, -size, size)


def flux(gu, gv):
    cross_x = gu[1] * gv[2] - gu[2] * gv[1]
    cross_y = gu[2] * gv[0] - gu[0] * gv[2]
    cross_z = gu[0] * gv[1] - gu[1] * gv[0]
    inverse = 1.0 / jnp.sqrt(EPSILON_SQ + cross_x * cross_x + cross_y * cross_y + cross_z * cross_z)
    norm_u = gu[0] * gu[0] + gu[1] * gu[1] + gu[2] * gu[2]
    norm_v = gv[0] * gv[0] + gv[1] * gv[1] + gv[2] * gv[2]
    inner = gu[0] * gv[0] + gu[1] * gv[1] + gu[2] * gv[2]
    flux_u = [(norm_v * gu[d] - inner * gv[d]) * inverse for d in range(3)]
    flux_v = [(norm_u * gv[d] - inner * gu[d]) * inverse for d in range(3)]
    return flux_u, flux_v


def dot(a, b, dims):
    return lax.dot_general(a, b, (dims, ((), ())), preferred_element_type=F32)


NN = ((1,), (0,))
NT = ((1,), (1,))


def kernel(
    act_hbm, ana_hbm, mr_hbm, sens_hbm, blocks_hbm, ids_hbm, counts_hbm, back_hbm,
    u_out, v_out,
    u_ref, v_ref, mr_ref, sens_ref, blk, ids_ref, counts_ref, back_ref,
    gather_ref, scatter_ref, full, picked, expect, ratio, back_terms, own_part,
    send_b, recv_b, send_h, recv_h, strip,
    load_sem, a_send, a_recv, b_send, b_recv, h_send, h_recv, c_send, c_recv, across_sem,
):
    gx = lax.axis_index("gx")
    gy = lax.axis_index("gy")
    sub = lax.axis_index("sub")
    cx, cy = gy // 4, (gy % 4) * 2 + sub
    slab = gx * 2 + sub

    def peer(a, b):
        x, y = lax.rem(cx + a, NCX), lax.rem(cy + b, NCY)
        return (gx, x * 4 + y // 2, lax.rem(y, 2))

    def neighbour(ds, dg):
        other = around(slab + ds, SLABS)
        return (other // 2, around(gy + dg, NGY), lax.rem(other, 2))

    barrier = pltpu.get_barrier_semaphore()
    first_slab, last_slab = slab == 0, slab == SLABS - 1
    first_gy, last_gy = gy == 0, gy == NGY - 1
    side = 2 * sub - 1
    across = (neighbour(side, 0), neighbour(side, -side))
    before_next = jnp.logical_and(sub == 1, jnp.logical_not(last_slab))
    after_last = jnp.logical_and(sub == 0, jnp.logical_not(first_slab))
    for a, b in OFFSETS:
        pl.semaphore_signal(barrier, inc=1, device_id=peer(a, b), device_id_type=MESH)

    @pl.when(before_next)
    def _():
        for device in across:
            pl.semaphore_signal(barrier, inc=1, device_id=device, device_id_type=MESH)

    mine = pl.ds(sub * 4, 4)
    loads = [
        pltpu.make_async_copy(act_hbm.at[mine], u_ref, load_sem.at[0]),
        pltpu.make_async_copy(ana_hbm.at[mine], v_ref, load_sem.at[1]),
        pltpu.make_async_copy(ids_hbm, ids_ref, load_sem.at[2]),
        pltpu.make_async_copy(blocks_hbm, blk, load_sem.at[3]),
        pltpu.make_async_copy(counts_hbm, counts_ref, load_sem.at[4]),
        pltpu.make_async_copy(back_hbm, back_ref, load_sem.at[5]),
        pltpu.make_async_copy(mr_hbm.at[mine], mr_ref, load_sem.at[6]),
        pltpu.make_async_copy(sens_hbm.at[mine], sens_ref, load_sem.at[7]),
    ]
    for load in loads:
        load.start()

    own_rows = pl.ds(pl.multiple_of(cy * HALF, HALF), HALF)
    row_id = lax.broadcasted_iota(jnp.int32, (8, BRICK), 0)
    lane_id = lax.broadcasted_iota(jnp.int32, (8, BRICK), 1)

    def share(phase):
        for a, b in OFFSETS:
            pltpu.make_async_remote_copy(
                src_ref=full.at[phase, 0, own_rows], dst_ref=full.at[phase, a, own_rows],
                send_sem=a_send.at[phase, a], recv_sem=a_recv.at[phase, a],
                device_id=peer(a, b), device_id_type=MESH).start()

    def await_group(ref, a, sem):
        part = ref.at[pl.ds(0, ref.shape[0] * (NCY - 1) // NCY)] if a == 0 else ref
        pltpu.make_async_copy(part, part, sem).wait()

    def pack_halo(phase):
        for f, ref in enumerate((u_ref, v_ref)):
            send_h[phase, 0, f] = ref[0]
            send_h[phase, 1, f] = ref[3]
            for x in range(4):
                send_h[phase, 2, f, x:x + 1, :] = ref[x, 0:1, :]
                send_h[phase, 3, f, x:x + 1, :] = ref[x, 7:8, :]
            send_h[phase, 4, f, 0:1, :] = ref[3, 0:1, :]
            send_h[phase, 5, f, 0:1, :] = ref[0, 7:8, :]

    def halo_copies(phase):
        copies = []
        for i, (ds, dg) in enumerate(HALOS):
            copies.append(pltpu.make_async_remote_copy(
                src_ref=send_h.at[phase, i], dst_ref=recv_h.at[phase, i],
                send_sem=h_send.at[phase, i], recv_sem=h_recv.at[phase, i],
                device_id=neighbour(ds, dg), device_id_type=MESH))
        return copies

    def goes(i):
        ds = HALOS[i][0]
        return None if ds == 0 else jnp.logical_not(last_slab if ds > 0 else first_slab)

    def comes(i):
        ds = HALOS[i][0]
        return None if ds == 0 else jnp.logical_not(first_slab if ds > 0 else last_slab)

    def only_if(condition, act):
        if condition is None:
            act()
        else:
            pl.when(condition)(act)

    def start_halo(copies, condition=None):
        for i, copy in enumerate(copies):
            terms = [c for c in (condition, goes(i)) if c is not None]
            only_if(functools.reduce(jnp.logical_and, terms) if terms else None, copy.start)

    def gather_bricks(phase):
        total = None
        for a in (0, 1, 3, 2):
            await_group(full.at[phase, a], a, a_recv.at[phase, a])
            part = dot(gather_ref[a], full[phase, a], NN)
            total = part if total is None else total + part
        picked[...] = total.reshape(TILES, KP, BRICK)

    def only_row(values, k):
        return jnp.where(row_id == k, values, 0.0).astype(BF16)

    def project(step, carry):
        for inner in range(TOGETHER):
            t = step * TOGETHER + inner
            x = picked[t]
            lhs = jnp.concatenate([only_row(x, k) for k in range(K)], axis=1)
            rhs = jnp.concatenate([blk[t, k] for k in range(K)], axis=1)
            total = dot(lhs, rhs, NT)
            expect[pl.ds(t, 1), :] = jnp.sum(total, axis=0, keepdims=True)
        return carry

    def backproject(step, carry):
        for inner in range(TOGETHER):
            t = step * TOGETHER + inner
            r = jnp.broadcast_to(ratio[pl.ds(t, 1), :], (8, LORT))
            lhs = jnp.concatenate([only_row(r, k) for k in range(K)], axis=1)
            back_terms[t] = dot(lhs, blk[t].reshape(K * LORT, BRICK), NN)
        return carry

    def scatter_and_send(phase):
        terms = back_terms[...].reshape(ENTRIES_PAD, BRICK)
        high = terms.astype(BF16)
        low = (terms - high.astype(F32)).astype(BF16)
        for a in (2, 1, 3, 0):
            part = dot(scatter_ref[a], high, NN) + dot(scatter_ref[a], low, NN)
            send_b[phase, a] = encode(part)
            if a == 0:
                own_part[...] = part
            for x, b in OFFSETS:
                if x != a:
                    continue
                rows = pl.ds(pl.multiple_of(lax.rem(cy + b, NCY) * HALF, HALF), HALF)
                slot = b - 1 if a == 0 else b
                pltpu.make_async_remote_copy(
                    src_ref=send_b.at[phase, a, rows], dst_ref=recv_b.at[phase, a, slot],
                    send_sem=b_send.at[phase, a], recv_sem=b_recv.at[phase, a],
                    device_id=peer(a, b), device_id_type=MESH).start()

    def summed_gradient(phase):
        total = own_part[own_rows, :]
        for a in (0, 1, 3, 2):
            await_group(recv_b.at[phase, a], a, b_recv.at[phase, a])
            for slot in range(NCY - 1 if a == 0 else NCY):
                total = total + decode(recv_b[phase, a, slot])
        return total.reshape(4, 8, BRICK)

    def await_sends(sent, phase, sems):
        for a in range(NCX):
            await_group(sent.at[phase, a], a, sems.at[phase, a])

    def prior(phase, copies):
        for i, copy in enumerate(copies):
            only_if(comes(i), copy.wait_recv)

        def layers(f, ref):
            return [recv_h[phase, 1, f]] + [ref[x] for x in range(4)] + [recv_h[phase, 0, f]]

        def depth(f):
            return jnp.where(lane_id < BRICK - 1, pltpu.roll(f, BRICK - 1, 1) - f, 0.0)

        def gradient(all_layers, f, x):
            here, after = all_layers[x], all_layers[x + 1]
            along_x = after - here
            if x == 4:
                along_x = jnp.where(last_slab, 0.0, along_x)
            row = recv_h[phase, 4, f, 0:1, :] if x == 0 else recv_h[phase, 2, f, x - 1:x, :]
            shifted = jnp.where(row_id < 7, pltpu.roll(here, 7, 0), jnp.broadcast_to(row, (8, BRICK)))
            along_y = jnp.where(jnp.logical_and(last_gy, row_id == 7), 0.0, shifted - here)
            return along_x, along_y, depth(here)

        def before_gradient(f):
            here = recv_h[phase, 3, f]
            after = recv_h[phase, 5, f, 0:1, :]
            shifted = jnp.where(row_id < 3, pltpu.roll(here, 7, 0), jnp.broadcast_to(after, (8, BRICK)))
            along_x = jnp.where(jnp.logical_and(last_slab, row_id == 3), 0.0, shifted - here)
            return along_x, send_h[phase, 2, f] - here, depth(here)

        us, vs = layers(0, u_ref), layers(1, v_ref)
        parts = [flux(gradient(us, 0, x), gradient(vs, 1, x)) for x in range(5)]
        before = flux(before_gradient(0), before_gradient(1))
        result = []
        for f in range(2):
            strip[f] = before[f][1]
            found = []
            for x in range(1, 5):
                now = parts[x][f]
                prev_x = parts[x - 1][f][0]
                if x == 1:
                    prev_x = jnp.where(first_slab, 0.0, prev_x)
                row = jnp.broadcast_to(strip[f, x - 1:x, :], (8, BRICK))
                row = jnp.where(first_gy, 0.0, row)
                prev_y = jnp.where(row_id > 0, pltpu.roll(now[1], 1, 0), row)
                prev_z = jnp.where(lane_id > 0, pltpu.roll(now[2], 1, 1), 0.0)
                found.append((prev_x - now[0]) + (prev_y - now[1]) + (prev_z - now[2]))
            result.append(found)
        return result

    loads[2].wait()
    entry_t = lax.broadcasted_iota(jnp.int32, (TILES, KP, ENTRIES_PAD), 0)
    entry_k = lax.broadcasted_iota(jnp.int32, (TILES, KP, ENTRIES_PAD), 1)
    lanes = lax.broadcasted_iota(jnp.int32, (TILES, KP, ENTRIES_PAD), 2)
    by_tile = jnp.concatenate([ids_ref[...], jnp.zeros((KP - K, TILES), jnp.int32)], axis=0).astype(F32)
    tile_lane = lax.broadcasted_iota(jnp.int32, (TILES, KP, TILES), 2)
    tile_of = lax.broadcasted_iota(jnp.int32, (TILES, KP, TILES), 0)
    k_of = lax.broadcasted_iota(jnp.int32, (TILES, KP, TILES), 1)
    chosen = jnp.logical_and(tile_lane == tile_of, k_of < K)
    column = jnp.sum(jnp.where(chosen, by_tile[None] + 1.0, 0.0), axis=2, keepdims=True)
    as_row = jnp.where(entry_t * KP + entry_k == lanes, column, 0.0)
    as_row = jnp.sum(jnp.sum(as_row, axis=0), axis=0, keepdims=True).astype(jnp.int32) - 1
    column = column.astype(jnp.int32) - 1
    bricks = lax.broadcasted_iota(jnp.int32, (QUAD, ENTRIES_PAD), 0)
    for a in range(NCX):
        came_from = around(cx - a, NCX) * QUAD
        goes_to = lax.rem(cx + a, NCX) * QUAD
        gather_ref[a] = jnp.where(lanes + came_from == column, 1.0, 0.0).reshape(ENTRIES, QUAD).astype(BF16)
        scatter_ref[a] = jnp.where(bricks + goes_to == as_row, 1.0, 0.0).astype(BF16)
    back_terms[pl.ds(TILES, ENTRIES_PAD // KP - TILES)] = jnp.zeros((ENTRIES_PAD // KP - TILES, KP, BRICK), F32)
    send_h[...] = jnp.zeros_like(send_h)
    loads[0].wait()
    loads[1].wait()
    full[0, 0, own_rows, :] = u_ref[...].reshape(HALF, BRICK).astype(BF16)

    @pl.when(jnp.logical_not(after_last))
    def _():
        pl.semaphore_wait(barrier, len(OFFSETS))

    @pl.when(after_last)
    def _():
        pl.semaphore_wait(barrier, len(OFFSETS) + len(across))
        for device in across:
            pl.semaphore_signal(across_sem, inc=1, device_id=device, device_id_type=MESH)

    def swap(i, out):
        copy = pltpu.make_async_remote_copy(
            src_ref=out.at[mine], dst_ref=out.at[mine],
            send_sem=c_send.at[i], recv_sem=c_recv.at[i], device_id=(gx, gy, 1 - sub), device_id_type=MESH)
        copy.start()
        return copy

    halos = []
    for phase in range(ITERS):
        share(phase)
        pack_halo(phase)
        halo = halo_copies(phase)
        if phase == 0:
            start_halo(halo, jnp.logical_not(before_next))
        else:
            start_halo(halo)
        if phase == 0:
            for i in (3, 4, 5, 6, 7):
                loads[i].wait()
        gather_bricks(phase)
        if phase == 0:
            @pl.when(before_next)
            def _():
                pl.semaphore_wait(across_sem, len(across))

            start_halo(halo, before_next)
        lax.fori_loop(0, TILES // TOGETHER, project, 0)
        ratio[...] = 1.0 - counts_ref[...] / (expect[...] + back_ref[...])
        lax.fori_loop(0, TILES // TOGETHER, backproject, 0)
        scatter_and_send(phase)
        await_sends(full, phase, a_send)
        halos += halo
        prior_u, prior_v = prior(phase, halo)
        last = phase == ITERS - 1
        step = [u_ref[x] / sens_ref[x] for x in range(4)]
        for x in range(4):
            v = v_ref[x]
            new_v = v - TAU * (v - mr_ref[x] + BETA * prior_v[x])
            if last:
                v_out[sub * 4 + x] = new_v
            else:
                v_ref[x] = new_v
        if last:
            swaps = [swap(1, v_out)]
        gradient = summed_gradient(phase)
        for x in range(4):
            new_u = jnp.maximum(u_ref[x] - step[x] * (gradient[x] + BETA * prior_u[x]), FLOOR)
            if last:
                u_out[sub * 4 + x] = new_u
            else:
                u_ref[x] = new_u
        if not last:
            full[phase + 1, 0, own_rows, :] = u_ref[...].reshape(HALF, BRICK).astype(BF16)

    swaps.append(swap(0, u_out))
    for phase in range(ITERS):
        await_sends(send_b, phase, b_send)
    for i, copy in enumerate(halos):
        only_if(goes(i % len(HALOS)), copy.wait_send)
    for copy in swaps:
        copy.wait()


def local(activity, anatomy, mr_data, sensitivity, blocks, brick_ids, counts, background):
    groups = (ITERS, NCX)
    hbm = pl.BlockSpec(memory_space=pltpu.HBM)
    vmem = pl.BlockSpec(memory_space=pltpu.VMEM)
    half = (4, 8, BRICK)
    dma = pltpu.SemaphoreType.DMA
    operands = (activity, anatomy, mr_data, sensitivity, blocks, brick_ids.T, counts, background)
    return pl.pallas_call(
        kernel,
        out_shape=(jax.ShapeDtypeStruct(activity.shape, F32), jax.ShapeDtypeStruct(anatomy.shape, F32)),
        in_specs=[hbm] * 8,
        out_specs=(vmem, vmem),
        scratch_shapes=[
            pltpu.VMEM(half, F32), pltpu.VMEM(half, F32), pltpu.VMEM(half, F32), pltpu.VMEM(half, F32),
            pltpu.VMEM(blocks.shape, BF16),
            pltpu.VMEM((K, TILES), jnp.int32),
            pltpu.VMEM(counts.shape, F32), pltpu.VMEM(background.shape, F32),
            pltpu.VMEM((NCX, ENTRIES, QUAD), BF16),
            pltpu.VMEM((NCX, QUAD, ENTRIES_PAD), BF16),
            pltpu.VMEM((ITERS, NCX, QUAD, BRICK), BF16),
            pltpu.VMEM((TILES, KP, BRICK), F32),
            pltpu.VMEM((TILES, LORT), F32),
            pltpu.VMEM((TILES, LORT), F32),
            pltpu.VMEM((ENTRIES_PAD // KP, KP, BRICK), F32),
            pltpu.VMEM((QUAD, BRICK), F32),
            pltpu.VMEM((ITERS, NCX, QUAD, BRICK), jnp.int16),
            pltpu.VMEM((ITERS, NCX, NCY, HALF, BRICK), jnp.int16),
            pltpu.VMEM((ITERS, 6, 2, 8, BRICK), F32),
            pltpu.VMEM((ITERS, 6, 2, 8, BRICK), F32),
            pltpu.VMEM((2, 8, BRICK), F32),
            dma((8,)), dma(groups), dma(groups), dma(groups), dma(groups),
            dma((ITERS, 6)), dma((ITERS, 6)), dma((2,)), dma((2,)), pltpu.SemaphoreType.REGULAR,
        ],
        compiler_params=pltpu.CompilerParams(
            collective_id=0, has_side_effects=True, vmem_limit_bytes=32 * 1024 * 1024),
    )(*[pltpu.with_memory_space_constraint(x, pltpu.HBM) for x in operands])


def solution(mesh):
    image = P("gx", "gy", None)
    tiles = ("gx", "gy", "sub")
    in_specs = (image, image, image, image, P(tiles, None, None, None), P(tiles, None), P(tiles, None), P(tiles, None))
    return jax.shard_map(local, mesh=mesh, in_specs=in_specs, out_specs=(image, image), check_vma=False)
```

```python
import functools
import math

import jax
import jax.numpy as jnp
from jax import lax
from jax.experimental import pallas as pl
from jax.experimental.pallas import tpu as pltpu
from jax.sharding import PartitionSpec as P

ITERS = 2
EPSILON_SQ = 0.01
BETA = 0.2
TAU = 0.5
FLOOR = 0.05

MESH = pl.DeviceIdType.MESH
F32 = jnp.float32
BF16 = jnp.bfloat16

NCX, NCY = 4, 8
NGX, NGY = 16, 16
SLABS = 2 * NGX
TILES, K, LORT, BRICK = 24, 6, 128, 128
TOGETHER = 24
KP = 8
ENTRIES = TILES * KP
ENTRIES_PAD = 256
HALF = 32
QUAD = NCY * HALF

CODE_EPS = 1.0 / 64.0
CODE_MAX = 256.0
CODE_Q = 32766.0 / math.log1p(CODE_MAX / CODE_EPS)


def around(value, size):
    return lax.rem(value + size, size)


def offsets():
    every = [(a, b) for a in range(NCX) for b in range(NCY) if (a, b) != (0, 0)]
    return sorted(every, key=lambda p: -(min(p[0], NCX - p[0]) + min(p[1], NCY - p[1])))


OFFSETS = offsets()


HALOS = ((-1, 0), (1, 0), (0, -1), (0, 1), (1, -1), (-1, 1))


def encode(x):
    code = jnp.log(1.0 + jnp.abs(x) * (1.0 / CODE_EPS)) * CODE_Q + 0.5
    code = jnp.minimum(code, 32767.0)
    return jnp.where(x < 0.0, -code, code).astype(jnp.int32).astype(jnp.int16)


def decode(code):
    value = code.astype(jnp.int32).astype(F32)
    size = (jnp.exp(jnp.abs(value) * (1.0 / CODE_Q)) - 1.0) * CODE_EPS
    return jnp.where(value < 0.0, -size, size)


def flux(gu, gv):
    cross_x = gu[1] * gv[2] - gu[2] * gv[1]
    cross_y = gu[2] * gv[0] - gu[0] * gv[2]
    cross_z = gu[0] * gv[1] - gu[1] * gv[0]
    inverse = 1.0 / jnp.sqrt(EPSILON_SQ + cross_x * cross_x + cross_y * cross_y + cross_z * cross_z)
    norm_u = gu[0] * gu[0] + gu[1] * gu[1] + gu[2] * gu[2]
    norm_v = gv[0] * gv[0] + gv[1] * gv[1] + gv[2] * gv[2]
    inner = gu[0] * gv[0] + gu[1] * gv[1] + gu[2] * gv[2]
    flux_u = [(norm_v * gu[d] - inner * gv[d]) * inverse for d in range(3)]
    flux_v = [(norm_u * gv[d] - inner * gu[d]) * inverse for d in range(3)]
    return flux_u, flux_v


def dot(a, b, dims):
    return lax.dot_general(a, b, (dims, ((), ())), preferred_element_type=F32)


NN = ((1,), (0,))
NT = ((1,), (1,))


def kernel(
    act_hbm, ana_hbm, mr_hbm, sens_hbm, blocks_hbm, ids_hbm, counts_hbm, back_hbm,
    u_out, v_out,
    u_ref, v_ref, mr_ref, sens_ref, blk, ids_ref, counts_ref, back_ref,
    gather_ref, scatter_ref, full, picked, expect, ratio, back_terms, own_part,
    send_b, recv_b, send_h, recv_h, strip, act_all,
    load_sem, a_send, a_recv, b_send, b_recv, h_send, h_recv, c_send, c_recv, across_sem,
):
    gx = lax.axis_index("gx")
    gy = lax.axis_index("gy")
    sub = lax.axis_index("sub")
    cx, cy = gy // 4, (gy % 4) * 2 + sub
    slab = gx * 2 + sub

    def peer(a, b):
        x, y = lax.rem(cx + a, NCX), lax.rem(cy + b, NCY)
        return (gx, x * 4 + y // 2, lax.rem(y, 2))

    def neighbour(ds, dg):
        other = around(slab + ds, SLABS)
        return (other // 2, around(gy + dg, NGY), lax.rem(other, 2))

    barrier = pltpu.get_barrier_semaphore()
    first_slab, last_slab = slab == 0, slab == SLABS - 1
    first_gy, last_gy = gy == 0, gy == NGY - 1
    side = 2 * sub - 1
    across = (neighbour(side, 0), neighbour(side, -side))
    before_next = jnp.logical_and(sub == 1, jnp.logical_not(last_slab))
    after_last = jnp.logical_and(sub == 0, jnp.logical_not(first_slab))
    for a, b in OFFSETS:
        pl.semaphore_signal(barrier, inc=1, device_id=peer(a, b), device_id_type=MESH)

    @pl.when(before_next)
    def _():
        for device in across:
            pl.semaphore_signal(barrier, inc=1, device_id=device, device_id_type=MESH)

    mine = pl.ds(sub * 4, 4)
    loads = [
        pltpu.make_async_copy(act_hbm.at[mine], u_ref, load_sem.at[0]),
        pltpu.make_async_copy(ana_hbm.at[mine], v_ref, load_sem.at[1]),
        pltpu.make_async_copy(ids_hbm, ids_ref, load_sem.at[2]),
        pltpu.make_async_copy(blocks_hbm, blk, load_sem.at[3]),
        pltpu.make_async_copy(counts_hbm, counts_ref, load_sem.at[4]),
        pltpu.make_async_copy(back_hbm, back_ref, load_sem.at[5]),
        pltpu.make_async_copy(mr_hbm.at[mine], mr_ref, load_sem.at[6]),
        pltpu.make_async_copy(sens_hbm.at[mine], sens_ref, load_sem.at[7]),
        pltpu.make_async_copy(act_hbm, act_all, load_sem.at[8]),
    ]
    for load in loads:
        load.start()

    own_rows = pl.ds(pl.multiple_of(cy * HALF, HALF), HALF)
    pair_rows = pl.ds(pl.multiple_of(cy // 2 * (2 * HALF), 2 * HALF), 2 * HALF)
    row_id = lax.broadcasted_iota(jnp.int32, (8, BRICK), 0)
    lane_id = lax.broadcasted_iota(jnp.int32, (8, BRICK), 1)

    def share(phase):
        for a, b in OFFSETS:
            pltpu.make_async_remote_copy(
                src_ref=full.at[phase, 0, own_rows], dst_ref=full.at[phase, a, own_rows],
                send_sem=a_send.at[phase, a], recv_sem=a_recv.at[phase, a],
                device_id=peer(a, b), device_id_type=MESH).start()

    def share_first(phase):
        for d in (3, 2, 1, 0):
            for a in (2, 1, 3, 0):
                if (a, d) != (0, 0):
                    pltpu.make_async_remote_copy(
                        src_ref=full.at[phase, 0, pair_rows], dst_ref=full.at[phase, a, pair_rows],
                        send_sem=a_send.at[phase, a], recv_sem=a_recv.at[phase, a],
                        device_id=peer(a, NCY + side * d), device_id_type=MESH).start()

    def await_group(ref, a, sem, own=1):
        part = ref.at[pl.ds(0, ref.shape[0] * (NCY - own) // NCY)] if a == 0 else ref
        pltpu.make_async_copy(part, part, sem).wait()

    def pack_halo(phase):
        for f, ref in enumerate((u_ref, v_ref)):
            send_h[phase, 0, f] = ref[0]
            send_h[phase, 1, f] = ref[3]
            for x in range(4):
                send_h[phase, 2, f, x:x + 1, :] = ref[x, 0:1, :]
                send_h[phase, 3, f, x:x + 1, :] = ref[x, 7:8, :]
            send_h[phase, 4, f, 0:1, :] = ref[3, 0:1, :]
            send_h[phase, 5, f, 0:1, :] = ref[0, 7:8, :]

    def halo_copies(phase):
        copies = []
        for i, (ds, dg) in enumerate(HALOS):
            copies.append(pltpu.make_async_remote_copy(
                src_ref=send_h.at[phase, i], dst_ref=recv_h.at[phase, i],
                send_sem=h_send.at[phase, i], recv_sem=h_recv.at[phase, i],
                device_id=neighbour(ds, dg), device_id_type=MESH))
        return copies

    def goes(i):
        ds = HALOS[i][0]
        return None if ds == 0 else jnp.logical_not(last_slab if ds > 0 else first_slab)

    def comes(i):
        ds = HALOS[i][0]
        return None if ds == 0 else jnp.logical_not(first_slab if ds > 0 else last_slab)

    def only_if(condition, act):
        if condition is None:
            act()
        else:
            pl.when(condition)(act)

    def start_halo(copies, condition=None):
        for i, copy in enumerate(copies):
            terms = [c for c in (condition, goes(i)) if c is not None]
            only_if(functools.reduce(jnp.logical_and, terms) if terms else None, copy.start)

    def gather_bricks(phase):
        total = None
        for a in (0, 1, 3, 2):
            await_group(full.at[phase, a], a, a_recv.at[phase, a], own=2 if phase == 0 else 1)
            part = dot(gather_ref[a], full[phase, a], NN)
            total = part if total is None else total + part
        picked[...] = total.reshape(TILES, KP, BRICK)

    def only_row(values, k):
        return jnp.where(row_id == k, values, 0.0).astype(BF16)

    def spread_rows(values):
        rows = [jnp.concatenate([jnp.where(row_id == k, x, 0.0) for k in range(K)], axis=1) for x in values]
        return jnp.concatenate(rows, axis=0).astype(BF16)

    def project(step, carry):
        for inner in range(0, TOGETHER, 2):
            t = step * TOGETHER + inner
            rows = [jnp.concatenate([blk[t + i, k] for k in range(K)], axis=1) for i in range(2)]
            total = dot(spread_rows([picked[t], picked[t + 1]]), jnp.concatenate(rows, axis=0), NT)
            for i in range(2):
                part = total[8 * i:8 * i + 8, LORT * i:LORT * i + LORT]
                expect[pl.ds(t + i, 1), :] = jnp.sum(part, axis=0, keepdims=True)
        return carry

    def backproject(step, carry):
        for inner in range(0, TOGETHER, 2):
            t = step * TOGETHER + inner
            r = [jnp.broadcast_to(ratio[pl.ds(t + i, 1), :], (8, LORT)) for i in range(2)]
            columns = [blk[t + i].reshape(K * LORT, BRICK) for i in range(2)]
            total = dot(spread_rows(r), jnp.concatenate(columns, axis=1), NN)
            for i in range(2):
                back_terms[t + i] = total[8 * i:8 * i + 8, BRICK * i:BRICK * i + BRICK]
        return carry

    def scatter_and_send(phase):
        terms = back_terms[...].reshape(ENTRIES_PAD, BRICK)
        high = terms.astype(BF16)
        low = (terms - high.astype(F32)).astype(BF16)
        for a in (2, 1, 3, 0):
            part = dot(scatter_ref[a], high, NN) + dot(scatter_ref[a], low, NN)
            send_b[phase, a] = encode(part)
            if a == 0:
                own_part[...] = part
            for x, b in OFFSETS:
                if x != a:
                    continue
                rows = pl.ds(pl.multiple_of(lax.rem(cy + b, NCY) * HALF, HALF), HALF)
                slot = b - 1 if a == 0 else b
                pltpu.make_async_remote_copy(
                    src_ref=send_b.at[phase, a, rows], dst_ref=recv_b.at[phase, a, slot],
                    send_sem=b_send.at[phase, a], recv_sem=b_recv.at[phase, a],
                    device_id=peer(a, b), device_id_type=MESH).start()

    def summed_gradient(phase):
        total = own_part[own_rows, :]
        for a in (0, 1, 3, 2):
            await_group(recv_b.at[phase, a], a, b_recv.at[phase, a])
            for slot in range(NCY - 1 if a == 0 else NCY):
                total = total + decode(recv_b[phase, a, slot])
        return total.reshape(4, 8, BRICK)

    def await_sends(sent, phase, sems, own=1):
        for a in range(NCX):
            await_group(sent.at[phase, a], a, sems.at[phase, a], own)

    def prior(phase, copies):
        for i, copy in enumerate(copies):
            only_if(comes(i), copy.wait_recv)

        def layers(f, ref):
            return [recv_h[phase, 1, f]] + [ref[x] for x in range(4)] + [recv_h[phase, 0, f]]

        def depth(f):
            return jnp.where(lane_id < BRICK - 1, pltpu.roll(f, BRICK - 1, 1) - f, 0.0)

        def gradient(all_layers, f, x):
            here, after = all_layers[x], all_layers[x + 1]
            along_x = after - here
            if x == 4:
                along_x = jnp.where(last_slab, 0.0, along_x)
            row = recv_h[phase, 4, f, 0:1, :] if x == 0 else recv_h[phase, 2, f, x - 1:x, :]
            shifted = jnp.where(row_id < 7, pltpu.roll(here, 7, 0), jnp.broadcast_to(row, (8, BRICK)))
            along_y = jnp.where(jnp.logical_and(last_gy, row_id == 7), 0.0, shifted - here)
            return along_x, along_y, depth(here)

        def before_gradient(f):
            here = recv_h[phase, 3, f]
            after = recv_h[phase, 5, f, 0:1, :]
            shifted = jnp.where(row_id < 3, pltpu.roll(here, 7, 0), jnp.broadcast_to(after, (8, BRICK)))
            along_x = jnp.where(jnp.logical_and(last_slab, row_id == 3), 0.0, shifted - here)
            return along_x, send_h[phase, 2, f] - here, depth(here)

        us, vs = layers(0, u_ref), layers(1, v_ref)
        parts = [flux(gradient(us, 0, x), gradient(vs, 1, x)) for x in range(5)]
        before = flux(before_gradient(0), before_gradient(1))
        result = []
        for f in range(2):
            strip[f] = before[f][1]
            found = []
            for x in range(1, 5):
                now = parts[x][f]
                prev_x = parts[x - 1][f][0]
                if x == 1:
                    prev_x = jnp.where(first_slab, 0.0, prev_x)
                row = jnp.broadcast_to(strip[f, x - 1:x, :], (8, BRICK))
                row = jnp.where(first_gy, 0.0, row)
                prev_y = jnp.where(row_id > 0, pltpu.roll(now[1], 1, 0), row)
                prev_z = jnp.where(lane_id > 0, pltpu.roll(now[2], 1, 1), 0.0)
                found.append((prev_x - now[0]) + (prev_y - now[1]) + (prev_z - now[2]))
            result.append(found)
        return result

    loads[2].wait()
    entry_t = lax.broadcasted_iota(jnp.int32, (TILES, KP, ENTRIES_PAD), 0)
    entry_k = lax.broadcasted_iota(jnp.int32, (TILES, KP, ENTRIES_PAD), 1)
    lanes = lax.broadcasted_iota(jnp.int32, (TILES, KP, ENTRIES_PAD), 2)
    by_tile = jnp.concatenate([ids_ref[...], jnp.zeros((KP - K, TILES), jnp.int32)], axis=0).astype(F32)
    tile_lane = lax.broadcasted_iota(jnp.int32, (TILES, KP, TILES), 2)
    tile_of = lax.broadcasted_iota(jnp.int32, (TILES, KP, TILES), 0)
    k_of = lax.broadcasted_iota(jnp.int32, (TILES, KP, TILES), 1)
    chosen = jnp.logical_and(tile_lane == tile_of, k_of < K)
    column = jnp.sum(jnp.where(chosen, by_tile[None] + 1.0, 0.0), axis=2, keepdims=True)
    as_row = jnp.where(entry_t * KP + entry_k == lanes, column, 0.0)
    as_row = jnp.sum(jnp.sum(as_row, axis=0), axis=0, keepdims=True).astype(jnp.int32) - 1
    column = column.astype(jnp.int32) - 1
    bricks = lax.broadcasted_iota(jnp.int32, (QUAD, ENTRIES_PAD), 0)
    for a in range(NCX):
        came_from = around(cx - a, NCX) * QUAD
        goes_to = lax.rem(cx + a, NCX) * QUAD
        gather_ref[a] = jnp.where(lanes + came_from == column, 1.0, 0.0).reshape(ENTRIES, QUAD).astype(BF16)
        scatter_ref[a] = jnp.where(bricks + goes_to == as_row, 1.0, 0.0).astype(BF16)
    back_terms[pl.ds(TILES, ENTRIES_PAD // KP - TILES)] = jnp.zeros((ENTRIES_PAD // KP - TILES, KP, BRICK), F32)
    send_h[...] = jnp.zeros_like(send_h)
    loads[0].wait()
    loads[1].wait()
    loads[8].wait()
    full[0, 0, pair_rows, :] = act_all[...].reshape(2 * HALF, BRICK).astype(BF16)

    @pl.when(jnp.logical_not(after_last))
    def _():
        pl.semaphore_wait(barrier, len(OFFSETS))

    @pl.when(after_last)
    def _():
        pl.semaphore_wait(barrier, len(OFFSETS) + len(across))
        for device in across:
            pl.semaphore_signal(across_sem, inc=1, device_id=device, device_id_type=MESH)

    def swap(i, out):
        copy = pltpu.make_async_remote_copy(
            src_ref=out.at[mine], dst_ref=out.at[mine],
            send_sem=c_send.at[i], recv_sem=c_recv.at[i], device_id=(gx, gy, 1 - sub), device_id_type=MESH)
        copy.start()
        return copy

    halos = []
    for phase in range(ITERS):
        if phase == 0:
            share_first(phase)
        else:
            share(phase)
        pack_halo(phase)
        halo = halo_copies(phase)
        if phase == 0:
            start_halo(halo, jnp.logical_not(before_next))
        else:
            start_halo(halo)
        if phase == 0:
            for i in (3, 4, 5, 6, 7):
                loads[i].wait()
        gather_bricks(phase)
        if phase == 0:
            @pl.when(before_next)
            def _():
                pl.semaphore_wait(across_sem, len(across))

            start_halo(halo, before_next)
        lax.fori_loop(0, TILES // TOGETHER, project, 0)
        ratio[...] = 1.0 - counts_ref[...] / (expect[...] + back_ref[...])
        lax.fori_loop(0, TILES // TOGETHER, backproject, 0)
        scatter_and_send(phase)
        await_sends(full, phase, a_send, own=2 if phase == 0 else 1)
        halos += halo
        prior_u, prior_v = prior(phase, halo)
        last = phase == ITERS - 1
        step = [u_ref[x] / sens_ref[x] for x in range(4)]
        for x in range(4):
            v = v_ref[x]
            new_v = v - TAU * (v - mr_ref[x] + BETA * prior_v[x])
            if last:
                v_out[sub * 4 + x] = new_v
            else:
                v_ref[x] = new_v
        if last:
            swaps = [swap(1, v_out)]
        gradient = summed_gradient(phase)
        for x in range(4):
            new_u = jnp.maximum(u_ref[x] - step[x] * (gradient[x] + BETA * prior_u[x]), FLOOR)
            if last:
                u_out[sub * 4 + x] = new_u
            else:
                u_ref[x] = new_u
        if not last:
            full[phase + 1, 0, own_rows, :] = u_ref[...].reshape(HALF, BRICK).astype(BF16)

    swaps.append(swap(0, u_out))
    for phase in range(ITERS):
        await_sends(send_b, phase, b_send)
    for i, copy in enumerate(halos):
        only_if(goes(i % len(HALOS)), copy.wait_send)
    for copy in swaps:
        copy.wait()


def local(activity, anatomy, mr_data, sensitivity, blocks, brick_ids, counts, background):
    groups = (ITERS, NCX)
    hbm = pl.BlockSpec(memory_space=pltpu.HBM)
    vmem = pl.BlockSpec(memory_space=pltpu.VMEM)
    half = (4, 8, BRICK)
    dma = pltpu.SemaphoreType.DMA
    operands = (activity, anatomy, mr_data, sensitivity, blocks, brick_ids.T, counts, background)
    return pl.pallas_call(
        kernel,
        out_shape=(jax.ShapeDtypeStruct(activity.shape, F32), jax.ShapeDtypeStruct(anatomy.shape, F32)),
        in_specs=[hbm] * 8,
        out_specs=(vmem, vmem),
        scratch_shapes=[
            pltpu.VMEM(half, F32), pltpu.VMEM(half, F32), pltpu.VMEM(half, F32), pltpu.VMEM(half, F32),
            pltpu.VMEM(blocks.shape, BF16),
            pltpu.VMEM((K, TILES), jnp.int32),
            pltpu.VMEM(counts.shape, F32), pltpu.VMEM(background.shape, F32),
            pltpu.VMEM((NCX, ENTRIES, QUAD), BF16),
            pltpu.VMEM((NCX, QUAD, ENTRIES_PAD), BF16),
            pltpu.VMEM((ITERS, NCX, QUAD, BRICK), BF16),
            pltpu.VMEM((TILES, KP, BRICK), F32),
            pltpu.VMEM((TILES, LORT), F32),
            pltpu.VMEM((TILES, LORT), F32),
            pltpu.VMEM((ENTRIES_PAD // KP, KP, BRICK), F32),
            pltpu.VMEM((QUAD, BRICK), F32),
            pltpu.VMEM((ITERS, NCX, QUAD, BRICK), jnp.int16),
            pltpu.VMEM((ITERS, NCX, NCY, HALF, BRICK), jnp.int16),
            pltpu.VMEM((ITERS, 6, 2, 8, BRICK), F32),
            pltpu.VMEM((ITERS, 6, 2, 8, BRICK), F32),
            pltpu.VMEM((2, 8, BRICK), F32),
            pltpu.VMEM(activity.shape, F32),
            dma((9,)), dma(groups), dma(groups), dma(groups), dma(groups),
            dma((ITERS, 6)), dma((ITERS, 6)), dma((2,)), dma((2,)), pltpu.SemaphoreType.REGULAR,
        ],
        compiler_params=pltpu.CompilerParams(
            collective_id=0, has_side_effects=True, vmem_limit_bytes=32 * 1024 * 1024),
    )(*[pltpu.with_memory_space_constraint(x, pltpu.HBM) for x in operands])


def solution(mesh):
    image = P("gx", "gy", None)
    tiles = ("gx", "gy", "sub")
    in_specs = (image, image, image, image, P(tiles, None, None, None), P(tiles, None), P(tiles, None), P(tiles, None))
    return jax.shard_map(local, mesh=mesh, in_specs=in_specs, out_specs=(image, image), check_vma=False)
```

```python
import functools
import math

import jax
import jax.numpy as jnp
from jax import lax
from jax.experimental import pallas as pl
from jax.experimental.pallas import tpu as pltpu
from jax.sharding import PartitionSpec as P

ITERS = 2
EPSILON_SQ = 0.01
BETA = 0.2
TAU = 0.5
FLOOR = 0.05

MESH = pl.DeviceIdType.MESH
F32 = jnp.float32
BF16 = jnp.bfloat16

NCX, NCY = 4, 8
NGX, NGY = 16, 16
SLABS = 2 * NGX
TILES, K, LORT, BRICK = 24, 6, 128, 128
TOGETHER = 24
KP = 8
ENTRIES = TILES * KP
ENTRIES_PAD = 256
HALF = 32
QUAD = NCY * HALF

CODE_EPS = 1.0 / 64.0
CODE_MAX = 256.0
CODE_Q = 32766.0 / math.log1p(CODE_MAX / CODE_EPS)


def around(value, size):
    return lax.rem(value + size, size)


def offsets():
    every = [(a, b) for a in range(NCX) for b in range(NCY) if (a, b) != (0, 0)]
    return sorted(every, key=lambda p: -(min(p[0], NCX - p[0]) + min(p[1], NCY - p[1])))


OFFSETS = offsets()


HALOS = ((-1, 0), (1, 0), (0, -1), (0, 1), (1, -1), (-1, 1))


def encode(x):
    code = jnp.log(1.0 + jnp.abs(x) * (1.0 / CODE_EPS)) * CODE_Q + 0.5
    code = jnp.minimum(code, 32767.0)
    return jnp.where(x < 0.0, -code, code).astype(jnp.int32).astype(jnp.int16)


def decode(code):
    value = code.astype(jnp.int32).astype(F32)
    size = (jnp.exp(jnp.abs(value) * (1.0 / CODE_Q)) - 1.0) * CODE_EPS
    return jnp.where(value < 0.0, -size, size)


def flux(gu, gv):
    cross_x = gu[1] * gv[2] - gu[2] * gv[1]
    cross_y = gu[2] * gv[0] - gu[0] * gv[2]
    cross_z = gu[0] * gv[1] - gu[1] * gv[0]
    inverse = 1.0 / jnp.sqrt(EPSILON_SQ + cross_x * cross_x + cross_y * cross_y + cross_z * cross_z)
    norm_u = gu[0] * gu[0] + gu[1] * gu[1] + gu[2] * gu[2]
    norm_v = gv[0] * gv[0] + gv[1] * gv[1] + gv[2] * gv[2]
    inner = gu[0] * gv[0] + gu[1] * gv[1] + gu[2] * gv[2]
    flux_u = [(norm_v * gu[d] - inner * gv[d]) * inverse for d in range(3)]
    flux_v = [(norm_u * gv[d] - inner * gu[d]) * inverse for d in range(3)]
    return flux_u, flux_v


def dot(a, b, dims):
    return lax.dot_general(a, b, (dims, ((), ())), preferred_element_type=F32)


NN = ((1,), (0,))
NT = ((1,), (1,))


def kernel(
    act_hbm, ana_hbm, mr_hbm, sens_hbm, blocks_hbm, ids_hbm, counts_hbm, back_hbm,
    u_out, v_out,
    u_ref, v_ref, mr_ref, sens_ref, blk, ids_ref, counts_ref, back_ref,
    gather_ref, scatter_ref, full, picked, expect, ratio, back_terms, own_part,
    send_b, recv_b, send_h, recv_h, strip, act_all,
    load_sem, a_send, a_recv, b_send, b_recv, h_send, h_recv, c_send, c_recv, across_sem,
):
    gx = lax.axis_index("gx")
    gy = lax.axis_index("gy")
    sub = lax.axis_index("sub")
    cx, cy = gy // 4, (gy % 4) * 2 + sub
    slab = gx * 2 + sub

    def peer(a, b):
        x, y = lax.rem(cx + a, NCX), lax.rem(cy + b, NCY)
        return (gx, x * 4 + y // 2, lax.rem(y, 2))

    def neighbour(ds, dg):
        other = around(slab + ds, SLABS)
        return (other // 2, around(gy + dg, NGY), lax.rem(other, 2))

    barrier = pltpu.get_barrier_semaphore()
    first_slab, last_slab = slab == 0, slab == SLABS - 1
    first_gy, last_gy = gy == 0, gy == NGY - 1
    side = 2 * sub - 1
    across = (neighbour(side, 0), neighbour(side, -side))
    before_next = jnp.logical_and(sub == 1, jnp.logical_not(last_slab))
    after_last = jnp.logical_and(sub == 0, jnp.logical_not(first_slab))
    for a, b in OFFSETS:
        pl.semaphore_signal(barrier, inc=1, device_id=peer(a, b), device_id_type=MESH)

    @pl.when(before_next)
    def _():
        for device in across:
            pl.semaphore_signal(barrier, inc=1, device_id=device, device_id_type=MESH)

    mine = pl.ds(sub * 4, 4)
    loads = [
        pltpu.make_async_copy(act_hbm.at[mine], u_ref, load_sem.at[0]),
        pltpu.make_async_copy(ana_hbm.at[mine], v_ref, load_sem.at[1]),
        pltpu.make_async_copy(ids_hbm, ids_ref, load_sem.at[2]),
        pltpu.make_async_copy(blocks_hbm, blk, load_sem.at[3]),
        pltpu.make_async_copy(counts_hbm, counts_ref, load_sem.at[4]),
        pltpu.make_async_copy(back_hbm, back_ref, load_sem.at[5]),
        pltpu.make_async_copy(mr_hbm.at[mine], mr_ref, load_sem.at[6]),
        pltpu.make_async_copy(sens_hbm.at[mine], sens_ref, load_sem.at[7]),
        pltpu.make_async_copy(act_hbm, act_all, load_sem.at[8]),
    ]
    for load in loads:
        load.start()

    own_rows = pl.ds(pl.multiple_of(cy * HALF, HALF), HALF)
    pair_rows = pl.ds(pl.multiple_of(cy // 2 * (2 * HALF), 2 * HALF), 2 * HALF)
    row_id = lax.broadcasted_iota(jnp.int32, (8, BRICK), 0)
    lane_id = lax.broadcasted_iota(jnp.int32, (8, BRICK), 1)

    def share(phase):
        for a, b in OFFSETS:
            pltpu.make_async_remote_copy(
                src_ref=full.at[phase, 0, own_rows], dst_ref=full.at[phase, a, own_rows],
                send_sem=a_send.at[phase, a], recv_sem=a_recv.at[phase, a],
                device_id=peer(a, b), device_id_type=MESH).start()

    def share_first(phase):
        for d in (3, 2, 1, 0):
            for a in (2, 1, 3, 0):
                if (a, d) != (0, 0):
                    pltpu.make_async_remote_copy(
                        src_ref=full.at[phase, 0, pair_rows], dst_ref=full.at[phase, a, pair_rows],
                        send_sem=a_send.at[phase, a], recv_sem=a_recv.at[phase, a],
                        device_id=peer(a, NCY + side * d), device_id_type=MESH).start()

    def await_group(ref, a, sem, own=1):
        part = ref.at[pl.ds(0, ref.shape[0] * (NCY - own) // NCY)] if a == 0 else ref
        pltpu.make_async_copy(part, part, sem).wait()

    def pack_halo(phase):
        for f, ref in enumerate((u_ref, v_ref)):
            send_h[phase, 0, f] = ref[0]
            send_h[phase, 1, f] = ref[3]
            for x in range(4):
                send_h[phase, 2, f, x:x + 1, :] = ref[x, 0:1, :]
                send_h[phase, 3, f, x:x + 1, :] = ref[x, 7:8, :]
            send_h[phase, 4, f, 0:1, :] = ref[3, 0:1, :]
            send_h[phase, 5, f, 0:1, :] = ref[0, 7:8, :]

    def halo_copies(phase):
        copies = []
        for i, (ds, dg) in enumerate(HALOS):
            copies.append(pltpu.make_async_remote_copy(
                src_ref=send_h.at[phase, i], dst_ref=recv_h.at[phase, i],
                send_sem=h_send.at[phase, i], recv_sem=h_recv.at[phase, i],
                device_id=neighbour(ds, dg), device_id_type=MESH))
        return copies

    def goes(i):
        ds = HALOS[i][0]
        return None if ds == 0 else jnp.logical_not(last_slab if ds > 0 else first_slab)

    def comes(i):
        ds = HALOS[i][0]
        return None if ds == 0 else jnp.logical_not(first_slab if ds > 0 else last_slab)

    def only_if(condition, act):
        if condition is None:
            act()
        else:
            pl.when(condition)(act)

    def start_halo(copies, condition=None):
        for i, copy in enumerate(copies):
            terms = [c for c in (condition, goes(i)) if c is not None]
            only_if(functools.reduce(jnp.logical_and, terms) if terms else None, copy.start)

    def gather_bricks(phase):
        total = None
        for a in (0, 1, 3, 2):
            await_group(full.at[phase, a], a, a_recv.at[phase, a], own=2 if phase == 0 else 1)
            part = dot(gather_ref[a], full[phase, a], NN)
            total = part if total is None else total + part
        picked[...] = total.reshape(TILES, KP, BRICK)

    def only_row(values, k):
        return jnp.where(row_id == k, values, 0.0).astype(BF16)

    def spread_rows(values):
        rows = [jnp.concatenate([jnp.where(row_id == k, x, 0.0) for k in range(K)], axis=1) for x in values]
        return jnp.concatenate(rows, axis=0).astype(BF16)

    def project(step, carry):
        for inner in range(0, TOGETHER, 2):
            t = step * TOGETHER + inner
            rows = [jnp.concatenate([blk[t + i, k] for k in range(K)], axis=1) for i in range(2)]
            total = dot(spread_rows([picked[t], picked[t + 1]]), jnp.concatenate(rows, axis=0), NT)
            for i in range(2):
                part = total[8 * i:8 * i + 8, LORT * i:LORT * i + LORT]
                expect[pl.ds(t + i, 1), :] = jnp.sum(part, axis=0, keepdims=True)
        return carry

    def backproject(step, carry):
        for inner in range(0, TOGETHER, 2):
            t = step * TOGETHER + inner
            r = [jnp.broadcast_to(ratio[pl.ds(t + i, 1), :], (8, LORT)) for i in range(2)]
            columns = [blk[t + i].reshape(K * LORT, BRICK) for i in range(2)]
            total = dot(spread_rows(r), jnp.concatenate(columns, axis=1), NN)
            for i in range(2):
                back_terms[t + i] = total[8 * i:8 * i + 8, BRICK * i:BRICK * i + BRICK]
        return carry

    def scatter_and_send(phase):
        terms = back_terms[...].reshape(ENTRIES_PAD, BRICK)
        high = terms.astype(BF16)
        low = (terms - high.astype(F32)).astype(BF16)
        for group in ((2,), (1, 3, 0)):
            for a in group:
                part = dot(scatter_ref[a], high, NN) + dot(scatter_ref[a], low, NN)
                send_b[phase, a] = encode(part)
                if a == 0:
                    own_part[...] = part
            for a in group:
                for x, b in OFFSETS:
                    if x != a:
                        continue
                    rows = pl.ds(pl.multiple_of(lax.rem(cy + b, NCY) * HALF, HALF), HALF)
                    slot = b - 1 if a == 0 else b
                    pltpu.make_async_remote_copy(
                        src_ref=send_b.at[phase, a, rows], dst_ref=recv_b.at[phase, a, slot],
                        send_sem=b_send.at[phase, a], recv_sem=b_recv.at[phase, a],
                        device_id=peer(a, b), device_id_type=MESH).start()

    def summed_gradient(phase):
        total = own_part[own_rows, :]
        for a in (0, 1, 3, 2):
            await_group(recv_b.at[phase, a], a, b_recv.at[phase, a])
            for slot in range(NCY - 1 if a == 0 else NCY):
                total = total + decode(recv_b[phase, a, slot])
        return total.reshape(4, 8, BRICK)

    def await_sends(sent, phase, sems, own=1):
        for a in range(NCX):
            await_group(sent.at[phase, a], a, sems.at[phase, a], own)

    def prior(phase, copies):
        for i, copy in enumerate(copies):
            only_if(comes(i), copy.wait_recv)

        def layers(f, ref):
            return [recv_h[phase, 1, f]] + [ref[x] for x in range(4)] + [recv_h[phase, 0, f]]

        def depth(f):
            return jnp.where(lane_id < BRICK - 1, pltpu.roll(f, BRICK - 1, 1) - f, 0.0)

        def gradient(all_layers, f, x):
            here, after = all_layers[x], all_layers[x + 1]
            along_x = after - here
            if x == 4:
                along_x = jnp.where(last_slab, 0.0, along_x)
            row = recv_h[phase, 4, f, 0:1, :] if x == 0 else recv_h[phase, 2, f, x - 1:x, :]
            shifted = jnp.where(row_id < 7, pltpu.roll(here, 7, 0), jnp.broadcast_to(row, (8, BRICK)))
            along_y = jnp.where(jnp.logical_and(last_gy, row_id == 7), 0.0, shifted - here)
            return along_x, along_y, depth(here)

        def before_gradient(f):
            here = recv_h[phase, 3, f]
            after = recv_h[phase, 5, f, 0:1, :]
            shifted = jnp.where(row_id < 3, pltpu.roll(here, 7, 0), jnp.broadcast_to(after, (8, BRICK)))
            along_x = jnp.where(jnp.logical_and(last_slab, row_id == 3), 0.0, shifted - here)
            return along_x, send_h[phase, 2, f] - here, depth(here)

        us, vs = layers(0, u_ref), layers(1, v_ref)
        parts = [flux(gradient(us, 0, x), gradient(vs, 1, x)) for x in range(5)]
        before = flux(before_gradient(0), before_gradient(1))
        result = []
        for f in range(2):
            strip[f] = before[f][1]
            found = []
            for x in range(1, 5):
                now = parts[x][f]
                prev_x = parts[x - 1][f][0]
                if x == 1:
                    prev_x = jnp.where(first_slab, 0.0, prev_x)
                row = jnp.broadcast_to(strip[f, x - 1:x, :], (8, BRICK))
                row = jnp.where(first_gy, 0.0, row)
                prev_y = jnp.where(row_id > 0, pltpu.roll(now[1], 1, 0), row)
                prev_z = jnp.where(lane_id > 0, pltpu.roll(now[2], 1, 1), 0.0)
                found.append((prev_x - now[0]) + (prev_y - now[1]) + (prev_z - now[2]))
            result.append(found)
        return result

    loads[2].wait()
    entry_t = lax.broadcasted_iota(jnp.int32, (TILES, KP, ENTRIES_PAD), 0)
    entry_k = lax.broadcasted_iota(jnp.int32, (TILES, KP, ENTRIES_PAD), 1)
    lanes = lax.broadcasted_iota(jnp.int32, (TILES, KP, ENTRIES_PAD), 2)
    by_tile = jnp.concatenate([ids_ref[...], jnp.zeros((KP - K, TILES), jnp.int32)], axis=0).astype(F32)
    tile_lane = lax.broadcasted_iota(jnp.int32, (TILES, KP, TILES), 2)
    tile_of = lax.broadcasted_iota(jnp.int32, (TILES, KP, TILES), 0)
    k_of = lax.broadcasted_iota(jnp.int32, (TILES, KP, TILES), 1)
    chosen = jnp.logical_and(tile_lane == tile_of, k_of < K)
    column = jnp.sum(jnp.where(chosen, by_tile[None] + 1.0, 0.0), axis=2, keepdims=True)
    as_row = jnp.where(entry_t * KP + entry_k == lanes, column, 0.0)
    as_row = jnp.sum(jnp.sum(as_row, axis=0), axis=0, keepdims=True).astype(jnp.int32) - 1
    column = column.astype(jnp.int32) - 1
    bricks = lax.broadcasted_iota(jnp.int32, (QUAD, ENTRIES_PAD), 0)
    for a in range(NCX):
        came_from = around(cx - a, NCX) * QUAD
        goes_to = lax.rem(cx + a, NCX) * QUAD
        gather_ref[a] = jnp.where(lanes + came_from == column, 1.0, 0.0).reshape(ENTRIES, QUAD).astype(BF16)
        scatter_ref[a] = jnp.where(bricks + goes_to == as_row, 1.0, 0.0).astype(BF16)
    back_terms[pl.ds(TILES, ENTRIES_PAD // KP - TILES)] = jnp.zeros((ENTRIES_PAD // KP - TILES, KP, BRICK), F32)
    send_h[...] = jnp.zeros_like(send_h)
    loads[0].wait()
    loads[1].wait()
    loads[8].wait()
    full[0, 0, pair_rows, :] = act_all[...].reshape(2 * HALF, BRICK).astype(BF16)

    @pl.when(jnp.logical_not(after_last))
    def _():
        pl.semaphore_wait(barrier, len(OFFSETS))

    @pl.when(after_last)
    def _():
        pl.semaphore_wait(barrier, len(OFFSETS) + len(across))
        for device in across:
            pl.semaphore_signal(across_sem, inc=1, device_id=device, device_id_type=MESH)

    def swap(i, out):
        copy = pltpu.make_async_remote_copy(
            src_ref=out.at[mine], dst_ref=out.at[mine],
            send_sem=c_send.at[i], recv_sem=c_recv.at[i], device_id=(gx, gy, 1 - sub), device_id_type=MESH)
        copy.start()
        return copy

    halos = []
    for phase in range(ITERS):
        if phase == 0:
            share_first(phase)
        else:
            share(phase)
        pack_halo(phase)
        halo = halo_copies(phase)
        if phase == 0:
            start_halo(halo, jnp.logical_not(before_next))
        else:
            start_halo(halo)
        if phase == 0:
            for i in (3, 4, 5, 6, 7):
                loads[i].wait()
        gather_bricks(phase)
        if phase == 0:
            @pl.when(before_next)
            def _():
                pl.semaphore_wait(across_sem, len(across))

            start_halo(halo, before_next)
        lax.fori_loop(0, TILES // TOGETHER, project, 0)
        ratio[...] = 1.0 - counts_ref[...] / (expect[...] + back_ref[...])
        lax.fori_loop(0, TILES // TOGETHER, backproject, 0)
        scatter_and_send(phase)
        await_sends(full, phase, a_send, own=2 if phase == 0 else 1)
        halos += halo
        prior_u, prior_v = prior(phase, halo)
        last = phase == ITERS - 1
        step = [u_ref[x] / sens_ref[x] for x in range(4)]
        for x in range(4):
            v = v_ref[x]
            new_v = v - TAU * (v - mr_ref[x] + BETA * prior_v[x])
            if last:
                v_out[sub * 4 + x] = new_v
            else:
                v_ref[x] = new_v
        if last:
            swaps = [swap(1, v_out)]
        gradient = summed_gradient(phase)
        for x in range(4):
            new_u = jnp.maximum(u_ref[x] - step[x] * (gradient[x] + BETA * prior_u[x]), FLOOR)
            if last:
                u_out[sub * 4 + x] = new_u
            else:
                u_ref[x] = new_u
        if not last:
            full[phase + 1, 0, own_rows, :] = u_ref[...].reshape(HALF, BRICK).astype(BF16)

    swaps.append(swap(0, u_out))
    for phase in range(ITERS):
        await_sends(send_b, phase, b_send)
    for i, copy in enumerate(halos):
        only_if(goes(i % len(HALOS)), copy.wait_send)
    for copy in swaps:
        copy.wait()


def local(activity, anatomy, mr_data, sensitivity, blocks, brick_ids, counts, background):
    groups = (ITERS, NCX)
    hbm = pl.BlockSpec(memory_space=pltpu.HBM)
    vmem = pl.BlockSpec(memory_space=pltpu.VMEM)
    half = (4, 8, BRICK)
    dma = pltpu.SemaphoreType.DMA
    operands = (activity, anatomy, mr_data, sensitivity, blocks, brick_ids.T, counts, background)
    return pl.pallas_call(
        kernel,
        out_shape=(jax.ShapeDtypeStruct(activity.shape, F32), jax.ShapeDtypeStruct(anatomy.shape, F32)),
        in_specs=[hbm] * 8,
        out_specs=(vmem, vmem),
        scratch_shapes=[
            pltpu.VMEM(half, F32), pltpu.VMEM(half, F32), pltpu.VMEM(half, F32), pltpu.VMEM(half, F32),
            pltpu.VMEM(blocks.shape, BF16),
            pltpu.VMEM((K, TILES), jnp.int32),
            pltpu.VMEM(counts.shape, F32), pltpu.VMEM(background.shape, F32),
            pltpu.VMEM((NCX, ENTRIES, QUAD), BF16),
            pltpu.VMEM((NCX, QUAD, ENTRIES_PAD), BF16),
            pltpu.VMEM((ITERS, NCX, QUAD, BRICK), BF16),
            pltpu.VMEM((TILES, KP, BRICK), F32),
            pltpu.VMEM((TILES, LORT), F32),
            pltpu.VMEM((TILES, LORT), F32),
            pltpu.VMEM((ENTRIES_PAD // KP, KP, BRICK), F32),
            pltpu.VMEM((QUAD, BRICK), F32),
            pltpu.VMEM((ITERS, NCX, QUAD, BRICK), jnp.int16),
            pltpu.VMEM((ITERS, NCX, NCY, HALF, BRICK), jnp.int16),
            pltpu.VMEM((ITERS, 6, 2, 8, BRICK), F32),
            pltpu.VMEM((ITERS, 6, 2, 8, BRICK), F32),
            pltpu.VMEM((2, 8, BRICK), F32),
            pltpu.VMEM(activity.shape, F32),
            dma((9,)), dma(groups), dma(groups), dma(groups), dma(groups),
            dma((ITERS, 6)), dma((ITERS, 6)), dma((2,)), dma((2,)), pltpu.SemaphoreType.REGULAR,
        ],
        compiler_params=pltpu.CompilerParams(
            collective_id=0, has_side_effects=True, vmem_limit_bytes=32 * 1024 * 1024),
    )(*[pltpu.with_memory_space_constraint(x, pltpu.HBM) for x in operands])


def solution(mesh):
    image = P("gx", "gy", None)
    tiles = ("gx", "gy", "sub")
    in_specs = (image, image, image, image, P(tiles, None, None, None), P(tiles, None), P(tiles, None), P(tiles, None))
    return jax.shard_map(local, mesh=mesh, in_specs=in_specs, out_specs=(image, image), check_vma=False)
```
